32 devices in a mesh: table: 4 (over x, core), row: 8 (over z, y).
Axes of the slice: x: 2, y: 2, z: 4, core: 2. Of those that a mesh axis runs over, the one named last changes fastest.
Arguments:
- cells: bfloat16 [4, 1024, 16, 192], P('table', 'row'), may hold values from -6 to 6
- missing: int32 [4, 1024, 16], P('table', 'row'), may hold values from 0 to 1
- train_counts: int32 [4], P('table'), may hold values from 256 to 768, as said below
- out_grad: bfloat16 [4, 1024, 16, 192], P('table', 'row'), may hold values from -6 to 6
- matrices: float32 [192, 2304], P(None, ('table', 'row')), may hold values from -4.131182 to 4.131182
- vectors: float32 [10, 192], replicated, may hold values from -4 to 4
- mat_first: float32 [192, 2304], P(None, ('table', 'row')), may hold values from -0.0024414062 to 0.0024414062
- mat_second: float32 [192, 2304], P(None, ('table', 'row')), may hold values from 2.2733001e-08 to 9.0932005e-08
- mat_average: float32 [192, 2304], P(None, ('table', 'row')), may hold values from -0.4375 to 0.4375
- vec_first: float32 [10, 192], replicated, may hold values from -0.009765625 to 0.009765625
- vec_second: float32 [10, 192], replicated, may hold values from 3.6372802e-07 to 1.4549121e-06
- vec_average: float32 [10, 192], replicated, may hold values from -4 to 4
Outputs:
- layer_out: bfloat16 [4, 1024, 16, 192], P('table', 'row')
- input_grad: bfloat16 [4, 1024, 16, 192], P('table', 'row')
- grad_norm: float32 [], replicated
- matrices_new: float32 [192, 2304], P(None, ('table', 'row'))
- matrices_first: float32 [192, 2304], P(None, ('table', 'row'))
- matrices_second: float32 [192, 2304], P(None, ('table', 'row'))
- matrices_average: float32 [192, 2304], P(None, ('table', 'row'))
- vectors_new: float32 [10, 192], replicated
- vectors_first: float32 [10, 192], replicated
- vectors_second: float32 [10, 192], replicated
- vectors_average: float32 [10, 192], replicated
The draws below stay inside these ranges and needn't reach their ends.
Inputs may be any that keep to these rules, and one draw needn't show every extreme that they name: `train_counts`: some table has exactly the least count and some table the largest.
All inputs are finite; a program needn't handle non-finite values.
Results may differ from the reference program's by a relative error of at most 0.02.
Values may be sent and summed in bfloat16 or wider, within the bound.
A program may use at most 320 MiB of HBM per device.

```python
import math
import jax
import jax.numpy as jnp
from jax import lax

D = 192
FFN = 384
HEADS = 6
HEAD_DIM = 32
ROWS = 1024
F = 16
STEP = 10
TABLES = 4
COLS = 2304


def draw_missing(key, part):
    level = jax.random.randint(jax.random.fold_in(key, 1), (TABLES, 1, F), 0, 6)
    drawn = jax.random.randint(jax.random.fold_in(key, 2), (TABLES, ROWS, F), 0, 64)
    limit = jnp.left_shift(jnp.ones_like(level), level)
    return (drawn < limit).astype(jnp.int32)


def draw_train_counts(key, part):
    least = ROWS // 4
    largest = 3 * ROWS // 4
    counts_drawn = jax.random.randint(jax.random.fold_in(key, 1), (TABLES,), least, largest + 1)
    order = jax.random.permutation(jax.random.fold_in(key, 2), TABLES)
    counts_drawn = counts_drawn.at[order[0]].set(largest)
    counts_drawn = counts_drawn.at[order[1]].set(least)
    return counts_drawn.astype(jnp.int32)


def draw_matrices(key, part):
    width_all = 8 * D + 2 * FFN
    entries = jax.random.truncated_normal(key, -4.0, 4.0, (D, width_all), jnp.float32)
    column = jnp.arange(width_all)
    plain = D ** (-0.5)
    factor = jnp.where(column < 3 * D, plain, jnp.where(column < 4 * D, (F / 3.0) ** 0.5 * plain, jnp.where(column < 7 * D, plain, jnp.where(column < 8 * D, (ROWS * 0.2) ** 0.5 * plain, jnp.where(column < 8 * D + FFN, plain, FFN ** (-0.5))))))
    return (entries * factor[None, :]).astype(jnp.float32)


def draw_vectors(key, part):
    entries = jax.random.truncated_normal(jax.random.fold_in(key, 1), -4.0, 4.0, (10, D), jnp.float32)
    gains = jax.random.uniform(jax.random.fold_in(key, 2), (10, D), jnp.float32, 0.5, 1.5)
    row = jnp.arange(10)[:, None]
    is_gain = (row == 1) | (row == 3) | (row == 5)
    result = jnp.where(row == 0, entries, jnp.where(is_gain, gains, 0.3 * entries))
    return result.astype(jnp.float32)


def level_of(rng, shape, split, low, top_value):
    factor_of = 1.0
    for position, shards_of in split:
        draws = jax.random.uniform(jax.random.fold_in(jax.random.fold_in(rng, 6), position), (shards_of,), jnp.float32, low / len(split), top_value / len(split))
        factor_of = factor_of * jnp.repeat(jnp.exp(draws), shape[position] // shards_of).reshape((-1,) + (1,) * (len(shape) - 1 - position))
    return factor_of


def bell_draw(key, shape, width, reach, cuts=(), kind=jnp.bfloat16):
    loudness = level_of(key, shape, cuts, -0.22, 0.18) if cuts else 1.0
    array = jax.random.normal(key, shape, jnp.float32) * width * loudness
    return jnp.minimum(jnp.maximum(array, -reach), reach).astype(kind)


def setup_inputs(seed: int = 0) -> dict:
    keys = jax.random.split(jax.random.key(seed), 13)
    cells = bell_draw(keys[0], (TABLES, ROWS, F, D), 1.0, 6.0, ((0, 4), (1, 8)))
    missing = draw_missing(jax.random.fold_in(keys[12], 71), 0)
    train_counts = draw_train_counts(jax.random.fold_in(keys[12], 71), 0)
    out_grad = bell_draw(keys[3], (TABLES, ROWS, F, D), 1.0, 6.0, ((0, 4), (1, 8)))
    matrices = draw_matrices(jax.random.fold_in(keys[12], 71), 0)
    vectors = draw_vectors(jax.random.fold_in(keys[12], 71), 0)
    mat_first = bell_draw(keys[6], (D, COLS), (0.11 * (D * (8 * D + 2 * FFN + 10)) ** -0.5), 0.0024414062, ((1, 32),), jnp.float32)
    mat_second = jnp.clip(jnp.exp(math.log(9.093200503684784e-08) - 1.3862944 * jax.random.uniform(keys[7], (D, COLS), jnp.float32) ** level_of(keys[7], (D, COLS), ((1, 32),), -0.2, 0.2)), 2.273300125921196e-08, 9.093200503684784e-08)
    mat_average = bell_draw(keys[8], (D, COLS), D ** -0.5, 0.4375, ((1, 32),), jnp.float32)
    vec_first = bell_draw(keys[9], (10, D), (0.44 * (D * (8 * D + 2 * FFN + 10)) ** -0.5), 0.009765625, (), jnp.float32)
    vec_second = jnp.clip(jnp.exp(jax.random.uniform(keys[10], (10, D), jnp.float32, math.log(3.6372802014739136e-07), math.log(1.4549120805895654e-06))), 3.6372802014739136e-07, 1.4549120805895654e-06)
    vec_average = bell_draw(keys[11], (10, D), 0.5, 4.0, (), jnp.float32)
    return dict(cells=cells, missing=missing, train_counts=train_counts, out_grad=out_grad, matrices=matrices, vectors=vectors, mat_first=mat_first, mat_second=mat_second, mat_average=mat_average, vec_first=vec_first, vec_second=vec_second, vec_average=vec_average)


@jax.custom_vjp
def low(v):
    return lax.optimization_barrier(v.astype(jnp.bfloat16)).astype(jnp.float32)

@jax.custom_vjp
def low_back(v):
    return v

def low_keep(v):
    return (low(v), None)

def low_pass(kept, grad):
    return (grad,)

def back_keep(v):
    return (v, None)

def back_low(kept, grad):
    return (low(grad),)
low.defvjp(low_keep, low_pass)
low_back.defvjp(back_keep, back_low)
exact_mode = lax.Precision.HIGHEST
norm_eps = 1e-05
row_mixer = 37
clip_limit = 1.0
learn_rate = 0.1
vector_rate = 0.5
beta_one = 0.9
beta_two = 0.99
adam_eps = 1e-08
decay_rate = 0.01
ema_rate = 0.9

def layer_norm(resid, gain, shift):
    center = resid - lax.optimization_barrier(jnp.mean(resid, -1, keepdims=True))
    spread = lax.optimization_barrier(jnp.mean(center * center, -1, keepdims=True))
    return center * lax.rsqrt(spread + norm_eps) * gain + shift

def attention(queries, keyset, valueset, usable):
    factor = HEAD_DIM ** (-0.5)
    scores = low_back(jnp.einsum('bqhe,bkhe->bhqk', queries, keyset, precision=exact_mode) * factor)
    scores = jnp.where(usable, scores, -1e+30)
    highest = lax.optimization_barrier(jnp.max(scores, -1, keepdims=True))
    exponent = jnp.exp(scores - highest)
    probability = low(exponent / lax.optimization_barrier(jnp.sum(exponent, -1, keepdims=True)))
    return low_back(low(jnp.einsum('bhqk,bkhe->bqhe', probability, valueset, precision=exact_mode)))

def project(values, weights):
    return jnp.einsum('rfd,dc->rfc', values, weights, precision=exact_mode)

def table_forward(table_cells, table_missing, table_train, weights, vecs):
    absent = table_missing[..., None] > 0
    embedded = low(jnp.where(absent, vecs[0], table_cells))
    first_proj = low_back(low(project(embedded, weights[:, :3 * D]))).reshape(ROWS, F, 3, HEADS, HEAD_DIM)
    every_key = jnp.ones((F,), dtype=bool)
    feature_out = attention(first_proj[:, :, 0], first_proj[:, :, 1], first_proj[:, :, 2], every_key)
    branch_one = low_back(project(feature_out.reshape(ROWS, F, D), weights[:, 3 * D:4 * D]))
    normed_one = low(layer_norm(embedded + branch_one, vecs[1], vecs[2]))
    second_proj = low_back(low(project(normed_one, weights[:, 4 * D:7 * D]))).reshape(ROWS, F, 3, HEADS, HEAD_DIM)
    columns = jnp.moveaxis(second_proj, 1, 0)
    row_ids = jnp.arange(ROWS, dtype=jnp.int32)
    usable = row_ids * row_mixer % ROWS < table_train

    def one_column(block):
        return attention(block[None, :, 0], block[None, :, 1], block[None, :, 2], usable)[0]
    item_out = jnp.moveaxis(lax.map(jax.checkpoint(one_column), columns), 0, 1)
    branch_two = low_back(project(item_out.reshape(ROWS, F, D), weights[:, 7 * D:8 * D]))
    normed_two = low(layer_norm(normed_one + branch_two, vecs[3], vecs[4]))
    hidden_in = low_back(project(normed_two, weights[:, 8 * D:8 * D + FFN]) + vecs[8:10].reshape(FFN))
    activated = low(jax.nn.gelu(hidden_in, approximate=True))
    branch_three = low_back(jnp.einsum('rfu,du->rfd', activated, weights[:, 8 * D + FFN:], precision=exact_mode) + vecs[7])
    return layer_norm(normed_two + branch_three, vecs[5], vecs[6])

def adam_step(param, grad, first, second, average, rate):
    first_new = beta_one * first + (1.0 - beta_one) * grad
    second_new = beta_two * second + (1.0 - beta_two) * grad * grad
    first_hat = first_new / (1.0 - beta_one ** STEP)
    second_hat = second_new / (1.0 - beta_two ** STEP)
    param_new = param - rate * (first_hat / (jnp.sqrt(second_hat) + adam_eps) + decay_rate * param)
    average_new = ema_rate * average + (1.0 - ema_rate) * param_new
    return (param_new, first_new, second_new, average_new)

def reference(cells, missing, train_counts, out_grad, matrices, vectors, mat_first, mat_second, mat_average, vec_first, vec_second, vec_average):
    cell_values = cells.astype(jnp.float32)
    cotangent = out_grad.astype(jnp.float32)

    def forward(mats, vecs, inputs):
        weights = low(mats)

        def one_table(pieces):
            return table_forward(pieces[0], pieces[1], pieces[2], weights, vecs)
        return lax.map(jax.checkpoint(one_table), (inputs, missing, train_counts))
    result, pullback = jax.vjp(forward, matrices, vectors, cell_values)
    grad_mats, grad_vecs, grad_cells = pullback(cotangent)
    grad_norm = jnp.sqrt(jnp.sum(grad_mats * grad_mats) + jnp.sum(grad_vecs * grad_vecs))
    factor = clip_limit / jnp.maximum(grad_norm, clip_limit)
    mats_out = adam_step(matrices, grad_mats * factor, mat_first, mat_second, mat_average, learn_rate)
    vecs_out = adam_step(vectors, grad_vecs * factor, vec_first, vec_second, vec_average, vector_rate)
    return (result.astype(jnp.bfloat16), grad_cells.astype(jnp.bfloat16), grad_norm, mats_out[0], mats_out[1], mats_out[2], mats_out[3], vecs_out[0], vecs_out[1], vecs_out[2], vecs_out[3])
```

```python
import functools
import math

import jax
import jax.numpy as jnp
from jax import lax
from jax.experimental import pallas as pl
from jax.experimental.pallas import tpu as pltpu
from jax.sharding import PartitionSpec as P

D = 192
FFN = 384
HEADS = 6
HD = 32
ROWS = 1024
F = 16
STEP = 10
KEYS = ROWS * 3 // 4
GROUP = 16 * F

EPS = 1e-05
MIXER = 37
CLIP = 1.0
RATE = 0.1
VEC_RATE = 0.5
B1 = 0.9
B2 = 0.99
ADAM_EPS = 1e-08
DECAY = 0.01
EMA = 0.9
SCALE = HD ** (-0.5)
EXPC = SCALE * math.log2(math.e)
NEG = -1e30

bf16 = jnp.bfloat16
f32 = jnp.float32
MESH = pl.DeviceIdType.MESH
VMEM = pl.BlockSpec(memory_space=pltpu.VMEM)
NT_DIMS = (((1,), (1,)), ((), ()))


def mm(a, b):
    return jnp.dot(a, b, preferred_element_type=f32)


def mm_nt(a, b):
    return lax.dot_general(a, b, NT_DIMS, preferred_element_type=f32)


def iota(shape, dim):
    return lax.broadcasted_iota(jnp.int32, shape, dim)


def eye(rows, columns):
    return (iota((rows, columns), 0) == iota((rows, columns), 1)).astype(bf16)


def ln_forward(r):
    center = r - jnp.sum(r, 0, keepdims=True) * (1.0 / D)
    spread = jnp.sum(center * center, 0, keepdims=True) * (1.0 / D)
    rstd = lax.rsqrt(spread + EPS)
    return center * rstd, rstd


def ln_backward(dy, n, rstd, gain):
    dn = dy * gain
    mean_one = jnp.sum(dn, 0, keepdims=True) * (1.0 / D)
    mean_two = jnp.sum(dn * n, 0, keepdims=True) * (1.0 / D)
    return (dn - mean_one - n * mean_two) * rstd


def lane_fold(x):
    total = x[:, 0:128]
    for k in range(1, x.shape[1] // 128):
        total = total + x[:, 128 * k : 128 * (k + 1)]
    return total


def cell_order(fc):
    p = iota((GROUP, GROUP), 0)
    q = iota((GROUP, GROUP), 1)
    per = GROUP // fc
    parity = p // per
    owner = (p % per) // 16
    row = p % 16
    return (q == row * F + owner * fc + parity).astype(bf16)


def packed_lanes(fc):
    return 384 if fc == 2 else 256


def gather_kernel(nr, n, mat_ref, wt_ref, w_ref, recv, full, send_sem, recv_sem):
    width = mat_ref.shape[1]
    pad = recv.shape[1]
    me = lax.axis_index("table") * nr + lax.axis_index("row")
    barrier = pltpu.get_barrier_semaphore()

    def greet(k, _):
        p = lax.rem(me + k, n)
        pl.semaphore_signal(barrier, inc=1, device_id=(p // nr, lax.rem(p, nr)), device_id_type=MESH)
        return 0

    lax.fori_loop(1, n, greet, 0)
    recv[me] = mm_nt(eye(pad, width), mat_ref[...].astype(bf16)).astype(bf16)
    pl.semaphore_wait(barrier, n - 1)

    def copy(slot, p):
        return pltpu.make_async_remote_copy(
            src_ref=recv.at[slot],
            dst_ref=recv.at[slot],
            send_sem=send_sem.at[p],
            recv_sem=recv_sem.at[slot],
            device_id=(p // nr, lax.rem(p, nr)),
            device_id_type=MESH,
        )

    def send(k, _):
        copy(me, lax.rem(me + k, n)).start()
        return 0

    lax.fori_loop(1, n, send, 0)

    def take(k, _):
        p = lax.rem(me + k, n)
        copy(p, p).wait_recv()
        return 0

    lax.fori_loop(1, n, take, 0)
    for p in range(n):
        full[p * width : (p + 1) * width, :] = recv[p].astype(f32)[0:width]
    wt = full[...].astype(bf16)
    wt_ref[...] = wt
    for k in range(wt.shape[0] // 128):
        w_ref[:, 128 * k : 128 * (k + 1)] = full[128 * k : 128 * (k + 1), :].T.astype(bf16)

    def sent(k, _):
        p = lax.rem(me + k, n)
        copy(me, p).wait_send()
        return 0

    lax.fori_loop(1, n, sent, 0)


def gather_weights(nr, n, matrices):
    width = matrices.shape[1]
    pad = -(-width // 16) * 16
    return pl.pallas_call(
        functools.partial(gather_kernel, nr, n),
        out_shape=[
            jax.ShapeDtypeStruct((width * n, D), bf16),
            jax.ShapeDtypeStruct((D, width * n), bf16),
        ],
        in_specs=[VMEM],
        out_specs=[VMEM, VMEM],
        scratch_shapes=[
            pltpu.VMEM((n, pad, D), bf16),
            pltpu.VMEM((width * n, D), f32),
            pltpu.SemaphoreType.DMA((n,)),
            pltpu.SemaphoreType.DMA((n,)),
        ],
        name="gather",
        compiler_params=pltpu.CompilerParams(
            collective_id=0, has_side_effects=True, vmem_limit_bytes=32 * 2**20
        ),
    )(matrices)


def swap_kernel(nr, count, *refs):
    ins, outs = refs[:count], refs[count : 2 * count]
    send_sem, recv_sem, own_sem = refs[2 * count :]
    t = lax.axis_index("table")
    me = lax.axis_index("row")
    barrier = pltpu.get_barrier_semaphore()

    def greet(k, _):
        pl.semaphore_signal(
            barrier, inc=1, device_id=(t, lax.rem(me + k, nr)), device_id_type=MESH
        )
        return 0

    lax.fori_loop(1, nr, greet, 0)
    pl.semaphore_wait(barrier, nr - 1)

    def copy(i, src, dst, p):
        return pltpu.make_async_remote_copy(
            src_ref=ins[i].at[src],
            dst_ref=outs[i].at[dst],
            send_sem=send_sem.at[i, src],
            recv_sem=recv_sem.at[i, dst],
            device_id=(t, p),
            device_id_type=MESH,
        )

    for i in range(count):

        def send(k, _):
            p = lax.rem(me + k, nr)
            copy(i, p, me, p).start()
            return 0

        lax.fori_loop(1, nr, send, 0)
    own = [pltpu.make_async_copy(ins[i].at[me], outs[i].at[me], own_sem.at[i]) for i in range(count)]
    for c in own:
        c.start()
    for c in own:
        c.wait()
    for i in range(count):

        def take(k, _):
            p = lax.rem(me + k, nr)
            copy(i, p, p, p).wait_recv()
            return 0

        lax.fori_loop(1, nr, take, 0)

        def sent(k, _):
            p = lax.rem(me + k, nr)
            copy(i, p, me, p).wait_send()
            return 0

        lax.fori_loop(1, nr, sent, 0)


def swap(nr, cid, *arrays):
    count = len(arrays)
    return pl.pallas_call(
        functools.partial(swap_kernel, nr, count),
        out_shape=[jax.ShapeDtypeStruct(a.shape, a.dtype) for a in arrays],
        in_specs=[VMEM] * count,
        out_specs=[VMEM] * count,
        scratch_shapes=[
            pltpu.SemaphoreType.DMA((count, nr)),
            pltpu.SemaphoreType.DMA((count, nr)),
            pltpu.SemaphoreType.DMA((count,)),
        ],
        name="swap%d" % cid,
        compiler_params=pltpu.CompilerParams(
            collective_id=cid, has_side_effects=True, vmem_limit_bytes=32 * 2**20
        ),
    )(*arrays)


def rows_forward_kernel(
    fc, cells, missing, og, vect, wt, qkv, o1, e, n1, rstd1, mask, expo, inv, hpack, gpack, order, qbd, kaug
):
    order[...] = cell_order(fc)
    lane = iota((16, 16 * HEADS * 8), 1)
    mask_rows = jnp.where(
        (iota((16, 128 * HEADS), 1) % 128) // F == iota((16, 128 * HEADS), 0), 0.0, NEG
    )
    qbd[0:D, :] = jnp.zeros((D, 128 * HEADS), bf16)
    qbd[D : D + 16, :] = mask_rows.astype(bf16)
    kaug[:, D : D + 16] = (iota((128, 16), 0) // F == iota((128, 16), 1)).astype(bf16)
    per = GROUP // fc
    owners = per // 16

    def group(g, _):
        at = pl.ds(pl.multiple_of(g * GROUP, GROUP), GROUP)
        rows = pl.ds(pl.multiple_of(g * 16, 16), 16)
        natural = cells[at, :]
        raw = mm_nt(eye(D, D), natural)
        spread = (iota((16, GROUP), 1) % F == iota((16, GROUP), 0)).astype(bf16)
        picked = mm(missing[rows, :].astype(f32).astype(bf16), spread)
        absent = jnp.sum(
            jnp.where(iota((16, GROUP), 1) // F == iota((16, GROUP), 0), picked, 0.0), 0, keepdims=True
        )
        mask[g] = absent
        et = jnp.where(absent > 0.5, vect[:, 0:1], raw).astype(bf16)
        e[g] = et
        proj = mm(wt[0 : 3 * D, :], et).astype(bf16)
        qkv[g] = proj
        outs = []
        for s in range(2):
            ln = slice(128 * s, 128 * (s + 1))
            for h in range(HEADS):
                qbd[HD * h : HD * (h + 1), 128 * h : 128 * (h + 1)] = proj[HD * h : HD * (h + 1), ln]
            kaug[:, 0:D] = proj[D : 2 * D, ln].astype(f32).T.astype(bf16)
            scores = mm(kaug[...], qbd[...])
            top = jnp.max(scores, 0, keepdims=True)
            ex = jnp.exp2((scores - top) * EXPC)
            total = jnp.sum(ex, 0, keepdims=True)
            exb = ex.astype(bf16)
            expo[2 * g + s] = exb
            recip = 1.0 / total
            inv[2 * g + s] = recip
            heads = []
            for h in range(HEADS):
                hl = slice(128 * h, 128 * (h + 1))
                heads.append(
                    mm(proj[2 * D + HD * h : 2 * D + HD * (h + 1), ln], exb[:, hl]) * recip[:, hl]
                )
            outs.append(jnp.concatenate(heads, 0))
        ot = jnp.concatenate(outs, 1).astype(bf16)
        o1[g] = ot
        r = et.astype(f32) + mm(wt[3 * D : 4 * D, :], ot)
        n, rstd = ln_forward(r)
        n1[g] = n
        rstd1[g] = rstd
        ht = (n * vect[:, 1:2] + vect[:, 2:3]).astype(bf16)
        lo = mm_nt(order[...], ht[0:128]).astype(bf16)
        ogn = og[at, :]
        glo = mm(order[...], ogn[:, 0:128]).astype(bf16)
        zero = jnp.zeros((64, GROUP), bf16)
        zero_n = jnp.zeros((GROUP, 64), bf16)
        hi_n = ogn[:, 128:D]
        if fc == 2:
            hi = mm_nt(order[0:per], jnp.concatenate([ht[128:D], zero], 0)) + mm_nt(
                order[per:], jnp.concatenate([zero, ht[128:D]], 0)
            )
            ghi = mm(order[0:per], jnp.concatenate([hi_n, zero_n], 1)) + mm(
                order[per:], jnp.concatenate([zero_n, hi_n], 1)
            )
        else:
            hi = mm_nt(order[...], jnp.concatenate([ht[128:D], zero], 0))
            ghi = mm(order[...], jnp.concatenate([hi_n, zero_n], 1))
        for c in range(fc):
            hpack[:, rows, 128 * c : 128 * (c + 1)] = lo[per * c : per * (c + 1)].reshape(owners, 16, 128)
            gpack[:, rows, 128 * c : 128 * (c + 1)] = glo[per * c : per * (c + 1)].reshape(owners, 16, 128)
        hpack[:, rows, 128 * fc :] = hi.astype(bf16).reshape(owners, 16, 128)
        gpack[:, rows, 128 * fc :] = ghi.astype(bf16).reshape(owners, 16, 128)
        return 0

    lax.fori_loop(0, cells.shape[0] // GROUP, group, 0)


def rows_forward(fc, nr, cells, missing, og, vect, wt):
    count = cells.shape[0]
    ng = count // GROUP
    lanes = packed_lanes(fc)
    sds = jax.ShapeDtypeStruct
    return pl.pallas_call(
        functools.partial(rows_forward_kernel, fc),
        out_shape=[
            sds((ng, 3 * D, GROUP), bf16),
            sds((ng, D, GROUP), bf16),
            sds((ng, D, GROUP), bf16),
            sds((ng, D, GROUP), f32),
            sds((ng, 1, GROUP), f32),
            sds((ng, 1, GROUP), f32),
            sds((2 * ng, 128, 128 * HEADS), bf16),
            sds((2 * ng, 1, 128 * HEADS), f32),
            sds((nr, ROWS // nr, lanes), bf16),
            sds((nr, ROWS // nr, lanes), bf16),
        ],
        in_specs=[VMEM] * 5,
        out_specs=[VMEM] * 10,
        scratch_shapes=[
            pltpu.VMEM((GROUP, GROUP), bf16),
            pltpu.VMEM((D + 16, 128 * HEADS), bf16),
            pltpu.VMEM((128, D + 16), bf16),
        ],
        name="rows_forward",
        compiler_params=pltpu.CompilerParams(vmem_limit_bytes=50 * 2**20),
    )(cells, missing, og, vect, wt)


def columns_kernel(
    fc,
    count_ref,
    hrecv,
    grecv,
    vect,
    wt,
    w,
    lo_out,
    dh_out,
    grads,
    vgrads,
    pick,
    x,
    xc,
    ht,
    ogt,
    ka,
    kvt,
    va,
    qa,
    da,
    ex,
    qt,
    ot,
    o2,
    n2,
    rstd2,
    h2b,
    gb,
    dub,
    dzb,
    da2b,
    dr2,
    dqb,
    dkvb,
    vacc,
):
    count = count_ref[0]
    pick[...] = (
        (iota((KEYS, ROWS), 1) * MIXER) % ROWS == iota((KEYS, ROWS), 0)
    ).astype(bf16)
    grads[...] = jnp.zeros(grads.shape, f32)
    vacc[...] = jnp.zeros(vacc.shape, f32)
    c0 = 4 * D
    lane_k = iota((KEYS, 128), 1)
    slot_k = iota((KEYS, 128), 0)
    extra = jnp.where(
        lane_k == 64,
        jnp.where(slot_k >= count, NEG, 0.0),
        jnp.where((lane_k == 65) | (lane_k == 66), 1.0, 0.0),
    )
    chunk = 256

    def column(col, _):
        def split(src, dst):
            if fc == 2:
                first = src[:, pl.ds(pl.multiple_of(col * 128, 128), 128)]
                tail = src[:, 256:384].astype(f32)
                tail = jnp.where(col == 0, tail, pltpu.roll(tail, 64, 1)).astype(bf16)
            else:
                first = src[:, 0:128]
                tail = src[:, 128:256]
            dst[:, 0:128] = first
            dst[:, 128:D] = tail[:, 0:64]

        split(hrecv, x)
        for c in range(ROWS // chunk):
            ht[:, c * chunk : (c + 1) * chunk] = mm_nt(eye(D, D), x[c * chunk : (c + 1) * chunk, :])
        for c in range(KEYS // 256):
            xc[c * 256 : (c + 1) * 256, :] = mm(pick[c * 256 : (c + 1) * 256, :], x[...]).astype(bf16)
        kvt[...] = mm_nt(wt[c0 + D : c0 + 3 * D, :], xc[...]).astype(bf16)
        proj_q = mm_nt(wt[c0 : c0 + D, :], x[...]).astype(bf16)
        qt[...] = proj_q
        ones16 = jnp.where(iota((16, ROWS), 0) == 0, 1.0, 0.0).astype(bf16)
        for h in range(HEADS):
            kv_rows = jnp.concatenate(
                [
                    wt[c0 + D + HD * h : c0 + D + HD * (h + 1), :],
                    wt[c0 + 2 * D + HD * h : c0 + 2 * D + HD * (h + 1), :],
                    jnp.zeros((64, D), bf16),
                ],
                0,
            )
            ka[h] = (mm_nt(xc[...], kv_rows) + extra).astype(bf16)
            va[h, 0:HD, :] = kvt[D + HD * h : D + HD * (h + 1), :]
            va[h, HD : HD + 16, :] = jnp.ones((16, KEYS), bf16)
            qa[h, 0:HD, :] = proj_q[HD * h : HD * (h + 1), :]
            qa[h, HD : 2 * HD, :] = jnp.zeros((HD, ROWS), bf16)
            qa[h, 2 * HD : 2 * HD + 16, :] = ones16

        def head_forward(h, _):
            for c in range(ROWS // 128):
                sl = slice(c * 128, (c + 1) * 128)
                s = mm(ka[h, :, 0:80], qa[h, :, sl])
                top = jnp.max(s, 0, keepdims=True)
                exb = jnp.exp2((s - top) * EXPC).astype(bf16)
                ex[h, :, sl] = exb
            for c in range(ROWS // 512):
                sl = slice(c * 512, (c + 1) * 512)
                o = mm(va[h], ex[h, :, sl])
                recip = 1.0 / o[HD : HD + 1]
                ot[h, 0:HD, sl] = o[0:HD] * recip
                ot[h, HD : HD + 8, sl] = jnp.broadcast_to(recip, (8, 512))
            return 0

        lax.fori_loop(0, HEADS, head_forward, 0)

        split(grecv, xc_og := ogt)

        def part(c, _):
            sl = pl.ds(pl.multiple_of(c * chunk, chunk), chunk)
            o_all = jnp.concatenate([ot[h, 0:HD, sl] for h in range(HEADS)], 0).astype(bf16)
            o2[:, sl] = o_all
            r2 = ht[:, sl] + mm(wt[7 * D : 8 * D, :], o_all)
            n, rstd = ln_forward(r2)
            n2[:, sl] = n
            rstd2[:, sl] = rstd
            h2 = (n * vect[:, 3:4] + vect[:, 4:5]).astype(bf16)
            h2b[:, sl] = h2
            bias = jnp.concatenate([vect[:, 8:9], vect[:, 9:10]], 0)
            u = mm(wt[8 * D : 8 * D + FFN, :], h2) + bias
            k0 = math.sqrt(2.0 / math.pi)
            usq = u * u
            th = jnp.tanh(k0 * u * (1.0 + 0.044715 * usq))
            g = (0.5 * u * (1.0 + th)).astype(bf16)
            slope = 0.5 * (1.0 + th) + 0.5 * u * (1.0 - th * th) * (k0 * (1.0 + 0.134145 * usq))
            gb[:, sl] = g
            r3 = h2.astype(f32) + mm(w[:, 8 * D + FFN :], g) + vect[:, 7:8]
            n3, rstd3 = ln_forward(r3)
            out = (n3 * vect[:, 5:6] + vect[:, 6:7]).astype(bf16)
            store_packed(out, lo_out, sl)
            up = mm_nt(eye(D, D), xc_og[sl, :])
            vacc[5] += lane_fold(up * n3)
            vacc[6] += lane_fold(up)
            dr3 = ln_backward(up, n3, rstd3, vect[:, 5:6])
            dz = dr3.astype(bf16)
            dzb[:, sl] = dz
            vacc[7] += lane_fold(dz.astype(f32))
            dg = mm(wt[8 * D + FFN :, :], dz)
            du = (slope * dg).astype(bf16)
            dub[:, sl] = du
            folded = lane_fold(du.astype(f32))
            vacc[8] += folded[0:D]
            vacc[9] += folded[D:]
            dh2 = dr3 + mm(w[:, 8 * D : 8 * D + FFN], du)
            vacc[3] += lane_fold(dh2 * n)
            vacc[4] += lane_fold(dh2)
            dr = ln_backward(dh2, n, rstd, vect[:, 3:4])
            dr2[:, sl] = dr
            da2 = dr.astype(bf16)
            da2b[:, sl] = da2
            do = mm(w[:, 7 * D : 8 * D], da2).astype(bf16)
            for h in range(HEADS):
                recip = ot[h, HD : HD + 1, sl]
                scaled = (do[HD * h : HD * (h + 1)].astype(f32) * recip).astype(bf16)
                delta = -jnp.sum(scaled.astype(f32) * ot[h, 0:HD, sl], 0, keepdims=True)
                hi = delta.astype(bf16).astype(f32)
                row = iota((16, chunk), 0)
                tail = jnp.where(row == 1, hi, jnp.where(row == 2, delta - hi, 0.0))
                da[h, 0:HD, sl] = jnp.zeros((HD, chunk), bf16)
                da[h, HD : 2 * HD, sl] = scaled
                da[h, 2 * HD : 2 * HD + 16, sl] = tail.astype(bf16)
            return 0

        def store_packed(value, out, sl):
            n_rows = value.shape[1]
            ident = eye(n_rows, n_rows)
            first = mm_nt(ident, value[0:128]).astype(bf16)
            zero = jnp.zeros((64, n_rows), bf16)
            if fc == 2:
                out[sl, pl.ds(pl.multiple_of(col * 128, 128), 128)] = first
                upper = jnp.where(col == 0, value[128:D].astype(f32), 0.0).astype(bf16)
                lower = jnp.where(col == 1, value[128:D].astype(f32), 0.0).astype(bf16)
                tail = mm_nt(ident, jnp.concatenate([upper, lower], 0)).astype(bf16)
                keep = jnp.where(col == 0, 0.0, 1.0)
                out[sl, 256:384] = (out[sl, 256:384].astype(f32) * keep + tail.astype(f32)).astype(bf16)
            else:
                out[sl, 0:128] = first
                out[sl, 128:256] = mm_nt(ident, jnp.concatenate([value[128:D], zero], 0)).astype(bf16)

        if fc == 2:

            @pl.when(col == 0)
            def _():
                lo_out[:, 256:384] = jnp.zeros((ROWS, 128), bf16)
                dh_out[:, 256:384] = jnp.zeros((ROWS, 128), bf16)

        lax.fori_loop(0, ROWS // chunk, part, 0)
        grads[0:FFN, :] += jnp.zeros((FFN, D), f32)
        grads[4 * D : 4 * D + FFN, :] += mm_nt(dub[...], h2b[...])
        grads[4 * D + FFN : 4 * D + 2 * FFN, :] += mm_nt(gb[...], dzb[...])
        grads[3 * D : 4 * D, :] += mm_nt(da2b[...], o2[...])

        def head_backward(h, _):
            for c in range(ROWS // 256):
                sl = slice(c * 256, (c + 1) * 256)
                t = mm(ka[h, :, 0:80], da[h, :, sl])
                dv_part = mm_nt(da[h, HD : 2 * HD, sl], ex[h, :, sl])
                ds = ex[h, :, sl] * t.astype(bf16)
                dq = mm(kvt[pl.ds(pl.multiple_of(HD * h, HD), HD), :], ds) * SCALE
                dqb[pl.ds(pl.multiple_of(HD * h, HD), HD), sl] = dq.astype(bf16)
                dk_part = mm_nt(qa[h, 0:HD, sl], ds)
                if c == 0:
                    dk, dv = dk_part, dv_part
                else:
                    dk, dv = dk + dk_part, dv + dv_part
            dkvb[pl.ds(pl.multiple_of(HD * h, HD), HD), :] = (dk * SCALE).astype(bf16)
            dkvb[pl.ds(pl.multiple_of(D + HD * h, HD), HD), :] = dv.astype(bf16)
            return 0

        lax.fori_loop(0, HEADS, head_backward, 0)
        grads[0:D, :] += mm(dqb[...], x[...])
        grads[D : 3 * D, :] += mm(dkvb[...], xc[...])
        dkey = mm(w[:, c0 + D : c0 + 3 * D], dkvb[...]).astype(bf16)

        def finish(c, _):
            sl = pl.ds(pl.multiple_of(c * chunk, chunk), chunk)
            dh = dr2[:, sl] + mm(w[:, c0 : c0 + D], dqb[:, sl]) + mm(dkey, pick[:, sl])
            store_packed(dh.astype(bf16), dh_out, sl)
            return 0

        lax.fori_loop(0, ROWS // chunk, finish, 0)
        return 0

    lax.fori_loop(0, fc, column, 0)
    for v in range(3, 10):
        acc = vacc[v]
        high = acc.astype(bf16)
        low = (acc - high.astype(f32)).astype(bf16)
        ones = jnp.ones((16, 128), bf16)
        vgrads[v : v + 1, :] = (mm_nt(ones, high) + mm_nt(ones, low))[0:1]


def columns(fc, count, hrecv, grecv, vect, wt, w):
    sds = jax.ShapeDtypeStruct
    lanes = packed_lanes(fc)
    sv = pltpu.VMEM
    return pl.pallas_call(
        functools.partial(columns_kernel, fc),
        out_shape=[
            sds((ROWS, lanes), bf16),
            sds((ROWS, lanes), bf16),
            sds((4 * D + 2 * FFN, D), f32),
            sds((16, D), f32),
        ],
        in_specs=[pl.BlockSpec(memory_space=pltpu.SMEM)] + [VMEM] * 5,
        out_specs=[VMEM] * 4,
        scratch_shapes=[
            sv((KEYS, ROWS), bf16),
            sv((ROWS, D), bf16),
            sv((KEYS, D), bf16),
            sv((D, ROWS), f32),
            sv((ROWS, D), bf16),
            sv((HEADS, KEYS, 128), bf16),
            sv((2 * D, KEYS), bf16),
            sv((HEADS, HD + 16, KEYS), bf16),
            sv((HEADS, 80, ROWS), bf16),
            sv((HEADS, 80, ROWS), bf16),
            sv((HEADS, KEYS, ROWS), bf16),
            sv((D, ROWS), bf16),
            sv((HEADS, HD + 8, ROWS), f32),
            sv((D, ROWS), bf16),
            sv((D, ROWS), f32),
            sv((1, ROWS), f32),
            sv((D, ROWS), bf16),
            sv((FFN, ROWS), bf16),
            sv((FFN, ROWS), bf16),
            sv((D, ROWS), bf16),
            sv((D, ROWS), bf16),
            sv((D, ROWS), f32),
            sv((D, ROWS), bf16),
            sv((2 * D, KEYS), bf16),
            sv((16, D, 128), f32),
        ],
        name="columns",
        compiler_params=pltpu.CompilerParams(vmem_limit_bytes=56 * 2**20),
    )(count, hrecv, grecv, vect, wt, w)


def rows_backward_kernel(
    fc, lrecv, drecv, qkv, o1, e, n1, rstd1, mask, expo, inv, vect, wt, w, layer, igrad, grads, vgrads, order, qbd, dbd, vacc
):
    order[...] = cell_order(fc)
    per = GROUP // fc
    owners = per // 16
    qbd[...] = jnp.zeros(qbd.shape, bf16)
    dbd[...] = jnp.zeros(dbd.shape, bf16)
    vacc[...] = jnp.zeros(vacc.shape, f32)
    grads[...] = jnp.zeros(grads.shape, f32)

    def group(g, _):
        at = pl.ds(pl.multiple_of(g * GROUP, GROUP), GROUP)
        rows = pl.ds(pl.multiple_of(g * 16, 16), 16)
        got = lrecv[:, rows, :].reshape(per, lrecv.shape[2])
        first = tail = 0.0
        got_d = drecv[:, rows, :].reshape(per, lrecv.shape[2])
        dt = got_d.astype(f32).T.astype(bf16)
        d_first = d_tail = 0.0
        for c in range(fc):
            back = order[per * c : per * (c + 1), :].astype(f32).T.astype(bf16)
            first = first + mm(back, got[:, 128 * c : 128 * (c + 1)])
            part = mm(back, got[:, 128 * fc :])
            tail = tail + part[:, 64 * c : 64 * (c + 1)]
            d_first = d_first + mm(dt[128 * c : 128 * (c + 1)], order[per * c : per * (c + 1), :])
            d_tail = d_tail + mm(
                dt[128 * fc + 64 * c : 128 * fc + 64 * (c + 1)], order[per * c : per * (c + 1), :]
            )
        layer[at, 0:128] = first.astype(bf16)
        layer[at, 128:D] = tail.astype(bf16)
        dh = jnp.concatenate([d_first, d_tail], 0)
        n = n1[g]
        vacc[1] += lane_fold(dh * n)
        vacc[2] += lane_fold(dh)
        dr = ln_backward(dh, n, rstd1[g], vect[:, 1:2])
        da = dr.astype(bf16)
        ot = o1[g]
        grads[3 * D : 4 * D, :] += mm_nt(da, ot)
        do = mm(w[:, 3 * D : 4 * D], da).astype(bf16)
        proj = qkv[g]
        parts = []
        for s in range(2):
            ln = slice(128 * s, 128 * (s + 1))
            recip = inv[2 * g + s]
            exb = expo[2 * g + s]
            deltas = []
            for h in range(HEADS):
                hs = slice(HD * h, HD * (h + 1))
                hl = slice(128 * h, 128 * (h + 1))
                scaled = (do[hs, ln].astype(f32) * recip[:, hl]).astype(bf16)
                dbd[hs, hl] = scaled
                qbd[hs, hl] = proj[HD * h : HD * (h + 1), ln]
                deltas.append(jnp.sum(scaled.astype(f32) * ot[hs, ln].astype(f32), 0, keepdims=True))
            vn = proj[2 * D : 3 * D, ln].astype(f32).T.astype(bf16)
            t = mm(vn, dbd[...]) - jnp.concatenate(deltas, 1)
            ds = (exb.astype(f32) * t).astype(bf16)
            dqs = [
                mm(proj[D + HD * h : D + HD * (h + 1), ln], ds[:, 128 * h : 128 * (h + 1)])
                for h in range(HEADS)
            ]
            dq = jnp.concatenate(dqs, 0) * SCALE
            dk = mm_nt(qbd[...], ds) * SCALE
            dv = mm_nt(dbd[...], exb)
            parts.append(jnp.concatenate([dq, dk, dv], 0))
        dproj = jnp.concatenate(parts, 1).astype(bf16)
        grads[0 : 3 * D, :] += mm_nt(dproj, e[g])
        de = dr + mm(w[:, 0 : 3 * D], dproj)
        absent = mask[g] > 0.5
        vacc[0] += lane_fold(jnp.where(absent, de, 0.0))
        kept = jnp.where(absent, 0.0, de).astype(bf16)
        igrad[at, :] = mm_nt(eye(GROUP, GROUP), kept).astype(bf16)
        return 0

    lax.fori_loop(0, layer.shape[0] // GROUP, group, 0)
    for v in range(3):
        acc = vacc[v]
        high = acc.astype(bf16)
        low = (acc - high.astype(f32)).astype(bf16)
        ones = jnp.ones((16, 128), bf16)
        vgrads[v : v + 1, :] = (mm_nt(ones, high) + mm_nt(ones, low))[0:1]


def rows_backward(fc, lrecv, drecv, saved, vect, wt, w):
    sds = jax.ShapeDtypeStruct
    ng = saved[0].shape[0]
    return pl.pallas_call(
        functools.partial(rows_backward_kernel, fc),
        out_shape=[
            sds((ng * GROUP, D), bf16),
            sds((ng * GROUP, D), bf16),
            sds((4 * D, D), f32),
            sds((16, D), f32),
        ],
        in_specs=[VMEM] * 13,
        out_specs=[VMEM] * 4,
        scratch_shapes=[
            pltpu.VMEM((GROUP, GROUP), bf16),
            pltpu.VMEM((D, 128 * HEADS), bf16),
            pltpu.VMEM((D, 128 * HEADS), bf16),
            pltpu.VMEM((4, D, 128), f32),
        ],
        name="rows_backward",
        compiler_params=pltpu.CompilerParams(vmem_limit_bytes=56 * 2**20),
    )(lrecv, drecv, *saved, vect, wt, w)


def adam(param, grad, first, second, average, rate):
    first_new = B1 * first + (1.0 - B1) * grad
    second_new = B2 * second + (1.0 - B2) * grad * grad
    first_hat = first_new * (1.0 / (1.0 - B1**STEP))
    second_hat = second_new * (1.0 / (1.0 - B2**STEP))
    param_new = param - rate * (first_hat / (jnp.sqrt(second_hat) + ADAM_EPS) + DECAY * param)
    average_new = EMA * average + (1.0 - EMA) * param_new
    return param_new, first_new, second_new, average_new


def update_kernel(nr, n, width, gone, gtwo, vone, vtwo, *refs):
    mats, vecs = refs[0:4], refs[4:8]
    norm_out = refs[8]
    mats_out, vecs_out = refs[9:13], refs[13:17]
    part, got, note, notes, send_sem, recv_sem, send_two, recv_two, full = refs[17:]
    pad = part.shape[1]
    me = lax.axis_index("table") * nr + lax.axis_index("row")
    barrier = pltpu.get_barrier_semaphore()

    def greet(k, _):
        p = lax.rem(me + k, n)
        pl.semaphore_signal(barrier, inc=1, device_id=(p // nr, lax.rem(p, nr)), device_id_type=MESH)
        return 0

    lax.fori_loop(1, n, greet, 0)
    split = gone.shape[0]
    full[0:split, :] = gone[...]
    full[split : split + gtwo.shape[0], :] = gtwo[...]
    full[split + gtwo.shape[0] :, :] = jnp.zeros((full.shape[0] - split - gtwo.shape[0], D), f32)
    vec = jnp.concatenate([vone[0:3, :], vtwo[3:10, :]], 0)
    spare = pad - width
    for p in range(n):
        block = full[p * width : p * width + pad, :]
        row = iota((pad, D), 0)
        block = jnp.where(row < width, block, 0.0)
        if p < 10:
            block = jnp.where(row == width, vec[p : p + 1, :], block)
        part[p] = block.astype(bf16)
    pl.semaphore_wait(barrier, n - 1)

    def copy(src, dst, p):
        return pltpu.make_async_remote_copy(
            src_ref=part.at[src],
            dst_ref=got.at[dst],
            send_sem=send_sem.at[src],
            recv_sem=recv_sem.at[dst],
            device_id=(p // nr, lax.rem(p, nr)),
            device_id_type=MESH,
        )

    def send(k, _):
        p = lax.rem(me + k, n)
        copy(p, me, p).start()
        return 0

    lax.fori_loop(1, n, send, 0)
    got[me] = part[me]

    def take(k, _):
        p = lax.rem(me + k, n)
        copy(p, p, p).wait_recv()
        return 0

    lax.fori_loop(1, n, take, 0)
    total = lax.fori_loop(0, n, lambda k, s: s + got[k].astype(f32), jnp.zeros((pad, D), f32))
    vec_row = total[width : width + 1, :]
    grad = jnp.where(iota((pad, D), 0) < width, total, 0.0)
    squares = jnp.sum(jnp.sum(grad * grad, 0, keepdims=True), 1, keepdims=True)
    first_row = iota((8, D), 0) == 0
    note[...] = jnp.where(first_row, vec_row, squares)
    notes[me] = note[...]

    def copy_two(dst, p):
        return pltpu.make_async_remote_copy(
            src_ref=note,
            dst_ref=notes.at[dst],
            send_sem=send_two.at[p],
            recv_sem=recv_two.at[dst],
            device_id=(p // nr, lax.rem(p, nr)),
            device_id_type=MESH,
        )

    def send_note(k, _):
        copy_two(me, lax.rem(me + k, n)).start()
        return 0

    lax.fori_loop(1, n, send_note, 0)
    wide = jnp.concatenate([grad, jnp.zeros((128 - pad, D), f32)], 0)
    wide = jnp.concatenate([wide, jnp.zeros((128, 256 - D), f32)], 1).T
    natural = wide[0:D, 0:width]

    def take_note(k, _):
        p = lax.rem(me + k, n)
        copy_two(p, p).wait_recv()
        return 0

    lax.fori_loop(1, n, take_note, 0)
    squares = lax.fori_loop(0, n, lambda k, s: s + notes[k, 1:2, 0:1], jnp.zeros((1, 1), f32))
    vec_total = jnp.concatenate([notes[p, 0:1, :] for p in range(10)], 0)
    squares = squares + jnp.sum(jnp.sum(vec_total * vec_total, 0, keepdims=True), 1, keepdims=True)
    norm = jnp.sqrt(squares)
    norm_out[...] = norm
    factor = CLIP / jnp.maximum(norm, CLIP)
    new = adam(mats[0][...], natural * factor, mats[1][...], mats[2][...], mats[3][...], RATE)
    for ref, value in zip(mats_out, new):
        ref[...] = value
    new = adam(vecs[0][...], vec_total * factor, vecs[1][...], vecs[2][...], vecs[3][...], VEC_RATE)
    for ref, value in zip(vecs_out, new):
        ref[...] = value

    def sent(k, _):
        p = lax.rem(me + k, n)
        copy(p, me, p).wait_send()
        copy_two(me, p).wait_send()
        return 0

    lax.fori_loop(1, n, sent, 0)


def update(nr, n, gone, gtwo, vone, vtwo, mats, vecs):
    width = mats[0].shape[1]
    pad = -(-(width + 1) // 16) * 16
    sds = jax.ShapeDtypeStruct
    return pl.pallas_call(
        functools.partial(update_kernel, nr, n, width),
        out_shape=[sds((1, 1), f32)] + [sds(m.shape, f32) for m in mats] + [sds(v.shape, f32) for v in vecs],
        in_specs=[VMEM] * 12,
        out_specs=[VMEM] * 9,
        scratch_shapes=[
            pltpu.VMEM((n, pad, D), bf16),
            pltpu.VMEM((n, pad, D), bf16),
            pltpu.VMEM((8, D), f32),
            pltpu.VMEM((n, 8, D), f32),
            pltpu.SemaphoreType.DMA((n,)),
            pltpu.SemaphoreType.DMA((n,)),
            pltpu.SemaphoreType.DMA((n,)),
            pltpu.SemaphoreType.DMA((n,)),
            pltpu.VMEM((width * n + 32, D), f32),
        ],
        name="update",
        compiler_params=pltpu.CompilerParams(
            collective_id=3, has_side_effects=True, vmem_limit_bytes=40 * 2**20
        ),
    )(gone, gtwo, vone, vtwo, *mats, *vecs)


def on_device(
    nr,
    n,
    cells,
    missing,
    train_counts,
    out_grad,
    matrices,
    vectors,
    mat_first,
    mat_second,
    mat_average,
    vec_first,
    vec_second,
    vec_average,
):
    fc = F // nr
    local = cells.shape[1]
    flat = cells.reshape(local * F, D)
    og = out_grad.reshape(local * F, D)
    vect = jnp.pad(vectors, ((0, 6), (0, 0))).T
    wt, w = gather_weights(nr, n, matrices)
    *saved, hpack, gpack = rows_forward(fc, nr, flat, missing[0], og, vect, wt)
    hrecv, grecv = swap(nr, 1, hpack, gpack)
    lanes = hpack.shape[2]
    lo, dh, gtwo, vtwo = columns(
        fc, train_counts, hrecv.reshape(ROWS, lanes), grecv.reshape(ROWS, lanes), vect, wt, w
    )
    lrecv, drecv = swap(nr, 2, lo.reshape(nr, ROWS // nr, lanes), dh.reshape(nr, ROWS // nr, lanes))
    layer, igrad, gone, vone = rows_backward(fc, lrecv, drecv, saved, vect, wt, w)
    norm, *rest = update(
        nr,
        n,
        gone,
        gtwo,
        vone,
        vtwo,
        (matrices, mat_first, mat_second, mat_average),
        (vectors, vec_first, vec_second, vec_average),
    )
    return (layer.reshape(cells.shape), igrad.reshape(cells.shape), norm[0, 0], *rest)


def solution(mesh):
    rows = P("table", "row", None, None)
    shard = P(None, ("table", "row"))
    nr = mesh.shape["row"]
    return jax.shard_map(
        functools.partial(on_device, nr, nr * mesh.shape["table"]),
        mesh=mesh,
        in_specs=(rows, P("table", "row", None), P("table"), rows, shard, P(), shard, shard, shard, P(), P(), P()),
        out_specs=(rows, rows, P(), shard, shard, shard, shard, P(), P(), P(), P()),
        check_vma=False,
    )
```

```python
import functools
import math

import jax
import jax.numpy as jnp
from jax import lax
from jax.experimental import pallas as pl
from jax.experimental.pallas import tpu as pltpu
from jax.sharding import PartitionSpec as P

D = 192
FFN = 384
HEADS = 6
HD = 32
ROWS = 1024
F = 16
STEP = 10
KEYS = ROWS * 3 // 4
COLS = 8 * D + 2 * FFN
SUB = 8
CELLS = SUB * F
WIDE = CELLS * HEADS
GAUG = D + 16
EAUG = D + 16
KAUG = 80
CHUNK = 256
SPAN = 512
CELLW = 1024

EPS = 1e-05
MIXER = 37
CLIP = 1.0
RATE = 0.1
VEC_RATE = 0.5
B1 = 0.9
B2 = 0.99
ADAM_EPS = 1e-08
DECAY = 0.01
EMA = 0.9
SCALE = HD ** (-0.5)
EXPC = SCALE * math.log2(math.e)
NEG = -1e30
GELU = math.sqrt(2.0 / math.pi)

QKV1, OUT1, QKV2, OUT2, UP, DOWN = 0, 3 * D, 4 * D, 7 * D, 8 * D, 8 * D + FFN

bf16 = jnp.bfloat16
f32 = jnp.float32
MESH = pl.DeviceIdType.MESH
VMEM = pl.BlockSpec(memory_space=pltpu.VMEM)
NT_DIMS = (((1,), (1,)), ((), ()))


def mm(a, b):
    return jnp.dot(a, b, preferred_element_type=f32)


def mm_nt(a, b):
    return lax.dot_general(a, b, NT_DIMS, preferred_element_type=f32)


def iota(shape, dim):
    return lax.broadcasted_iota(jnp.int32, shape, dim)


def eye(size):
    return (iota((size, size), 0) == iota((size, size), 1)).astype(bf16)


def ln_forward(r):
    center = r - jnp.sum(r, 0, keepdims=True) * (1.0 / D)
    spread = jnp.sum(center * center, 0, keepdims=True) * (1.0 / D)
    rstd = lax.rsqrt(spread + EPS)
    return center * rstd, rstd


def ln_backward(dy, n, rstd, gain):
    dn = dy * gain
    mean_one = jnp.sum(dn, 0, keepdims=True) * (1.0 / D)
    mean_two = jnp.sum(dn * n, 0, keepdims=True) * (1.0 / D)
    return (dn - mean_one - n * mean_two) * rstd


def fold(x):
    total = x[:, 0:128]
    for k in range(1, x.shape[1] // 128):
        total = total + x[:, 128 * k : 128 * (k + 1)]
    return total


def fit(x):
    if x.shape[1] >= 128:
        return fold(x)
    return jnp.concatenate([x, jnp.zeros((x.shape[0], 128 - x.shape[1]), x.dtype)], 1)


class Refs:
    def __init__(self, names, refs):
        for name, ref in zip(names, refs, strict=True):
            setattr(self, name, ref)


def embed(s, local):
    ident = eye(local)
    shade = s.vect[:, 0:1]

    def one(f, _):
        absent = s.missing[pl.ds(f, 1), :] > 0
        e = jnp.where(absent, shade, s.hs[f].astype(f32)).astype(bf16)
        s.et[f] = e
        flag = jnp.where((iota((16, local), 0) == 0) & absent, 1.0, 0.0).astype(bf16)
        s.nat[f] = mm_nt(ident, jnp.concatenate([e, flag], 0))
        return 0

    lax.fori_loop(0, F, one, 0, unroll=2)


def group_setup(s):
    same = jnp.where((iota((16, WIDE), 1) % SUB) == iota((16, WIDE), 0), 0.0, NEG).astype(bf16)
    hot = (iota((CELLS, 16), 0) % SUB == iota((CELLS, 16), 1)).astype(bf16)
    for k in range(2):
        s.qbd[k, 0:D, :] = jnp.zeros((D, WIDE), bf16)
        s.qbd[k, D:GAUG, :] = same
        s.dbd[k] = jnp.zeros((D, WIDE), bf16)
        s.dbd[k + 2] = jnp.zeros((D, WIDE), bf16)
    for g in range(s.vn.shape[0]):
        s.kaug[2 * g + 1, :, 64:80] = hot


def group_cells(ref, g):
    at = pl.ds(pl.multiple_of(g * SUB, SUB), SUB)
    return ref[:, at, :].reshape(CELLS, EAUG).astype(bf16)


def group_forward(s, local):
    ident = eye(CELLS)
    pairs = local // SUB // 2

    def project(i):
        eg = jnp.concatenate([group_cells(s.nat, 2 * i), group_cells(s.nat, 2 * i + 1)], 0)
        s.eg[pl.ds(pl.multiple_of(i * 2 * CELLS, 2 * CELLS), 2 * CELLS), :] = eg
        eg = eg[:, 0:D]
        proj = mm_nt(s.wt[QKV1 : QKV1 + 3 * D, :], eg).astype(bf16)
        kn = mm(eg, s.w[:, QKV1 + D : QKV1 + 3 * D]).astype(bf16)
        s.qkv[i] = proj
        for k in range(2):
            key = kn[CELLS * k : CELLS * (k + 1)]
            s.kaug[4 * i + 2 * k] = key[:, 0:128]
            s.kaug[4 * i + 2 * k + 1, :, 0:64] = key[:, 128:D]
            s.vn[2 * i + k] = kn[CELLS * k : CELLS * (k + 1), D:]

    def score(i, k):
        g = 2 * i + k
        at = slice(CELLS * k, CELLS * (k + 1))
        for h in range(HEADS):
            s.qbd[k, HD * h : HD * (h + 1), CELLS * h : CELLS * (h + 1)] = s.qkv[i, HD * h : HD * (h + 1), at]
        keys = jnp.concatenate([s.kaug[2 * g], s.kaug[2 * g + 1, :, 0:80]], 1)
        scores = mm(keys, s.qbd[k])
        top = jnp.max(scores, 0, keepdims=True)
        ex = jnp.exp2((scores - top) * EXPC)
        s.inv[g] = 1.0 / jnp.sum(ex, 0, keepdims=True)
        s.expo[g] = ex.astype(bf16)

    def result(i, k):
        g = 2 * i + k
        at = slice(CELLS * k, CELLS * (k + 1))
        heads = []
        for h in range(HEADS):
            hl = slice(CELLS * h, CELLS * (h + 1))
            value = s.qkv[i, 2 * D + HD * h : 2 * D + HD * (h + 1), at]
            heads.append(mm(value, s.expo[g, :, hl]) * s.inv[g, :, hl])
        o = jnp.concatenate(heads, 0).astype(bf16)
        s.og1[g] = o
        s.on[:, pl.ds(pl.multiple_of(g * SUB, SUB), SUB), :] = mm_nt(ident, o).reshape(F, SUB, D)

    def body(i, _):
        for k in range(2):
            result(i - 1, k)
        for k in range(2):
            score(i, k)
        project(i + 1)
        return 0

    project(0)
    for k in range(2):
        score(0, k)
    project(1)
    lax.fori_loop(1, pairs - 1, body, 0)
    for k in range(2):
        result(pairs - 2, k)
    for k in range(2):
        score(pairs - 1, k)
    for k in range(2):
        result(pairs - 1, k)


def rows_norm(s, f, per):
    local = s.et.shape[2]
    on = jnp.concatenate([s.on[f + k] for k in range(per)], 0).astype(bf16)
    e = jnp.concatenate([s.et[f + k] for k in range(per)], 1)
    r = e.astype(f32) + mm_nt(s.wt[OUT1 : OUT1 + D, :], on)
    n, rstd = ln_forward(r)
    h = (n * s.vect[:, 1:2] + s.vect[:, 2:3]).astype(bf16)
    for k in range(per):
        at = slice(local * k, local * (k + 1))
        s.n1[f + k] = n[:, at]
        s.rstd1[f + k] = rstd[:, at]
        s.hs[f + k] = h[:, at]


def make_pick(s):
    for c in range(ROWS // 128):
        slot = ((iota((128, KEYS), 0) + 128 * c) * MIXER) % ROWS
        s.pick[128 * c : 128 * (c + 1), :] = (slot == iota((128, KEYS), 1)).astype(bf16)


def column_project(s, col, nr):
    local = ROWS // nr
    count = s.count[0]
    for r in range(nr):
        s.xt[:, local * r : local * (r + 1)] = s.hr[r, col]
    s.xct[...] = mm(s.xt[...], s.pick[...]).astype(bf16)
    kvt = mm(s.wt[QKV2 + D : QKV2 + 3 * D, :], s.xct[...]).astype(bf16)
    s.kt[...] = kvt[0:D]
    q = mm(s.wt[QKV2 : QKV2 + D, :], s.xt[...]).astype(bf16)
    ident = eye(256)
    lane = iota((256, 128), 1)
    ones_v = jnp.where((lane == 0) | (lane == 1), 1.0, 0.0)
    first = jnp.where(iota((16, ROWS), 0) == 0, 1.0, 0.0).astype(bf16)
    for pair in range(HEADS // 2):
        h = 2 * pair
        stack = jnp.concatenate(
            [kvt[part + HD * k : part + HD * (k + 1)] for part in (0, D) for k in (h, h + 1)], 0
        )
        for c in range(KEYS // 256):
            at = slice(256 * c, 256 * (c + 1))
            both = mm_nt(ident, stack[:, at])
            bias = jnp.where((lane == 64) & (iota((256, 128), 0) + 256 * c >= count), NEG, 0.0)
            s.ka[pair, at, :] = jnp.where(lane < 64, both, bias).astype(bf16)
            s.vb[pair, at, :] = jnp.where(lane >= 64, both, ones_v).astype(bf16)
        for k in range(2):
            s.qa[h + k, 0:64, :] = jnp.zeros((64, ROWS), bf16)
            s.qa[h + k, HD * k : HD * (k + 1), :] = q[HD * (h + k) : HD * (h + k + 1), :]
            s.qa[h + k, 64:KAUG, :] = first
            s.va[h + k, 0:HD, :] = kvt[D + HD * (h + k) : D + HD * (h + k + 1)]
            s.va[h + k, HD : HD + 16, :] = jnp.ones((16, KEYS), bf16)


def column_forward(s):
    per = ROWS // SPAN
    steps = HEADS * per

    def place(i):
        return i // per, pl.ds(pl.multiple_of(lax.rem(i, per) * SPAN, SPAN), SPAN)

    def score(i, k):
        h, sl = place(i)
        sc = mm(s.ka[h // 2, :, 0:KAUG], s.qa[h, :, sl])
        s.sc[k] = sc
        s.top[k] = jnp.broadcast_to(jnp.max(sc, 0, keepdims=True), (8, SPAN))

    def weigh(i, k):
        h, sl = place(i)
        ex = jnp.exp2((s.sc[k] - s.top[k, 0:1]) * EXPC).astype(bf16)
        s.ex[h, :, sl] = ex
        o = mm(s.va[h], ex)
        recip = 1.0 / o[HD : HD + 1]
        s.ot[h, 0:HD, sl] = o[0:HD] * recip
        s.ot[h, HD : HD + 8, sl] = jnp.broadcast_to(recip, (8, SPAN))

    def body(i, _):
        score(2 * i + 1, 1)
        weigh(2 * i, 0)
        score(2 * i + 2, 0)
        weigh(2 * i + 1, 1)
        return 0

    score(0, 0)
    lax.fori_loop(0, steps // 2 - 1, body, 0)
    score(steps - 1, 1)
    weigh(steps - 2, 0)
    weigh(steps - 1, 1)


def keep_wide(s, c, width, value):
    for k in range(width // SPAN):
        s.sc[0, D * k : D * (k + 1), :] = value[:, SPAN * k : SPAN * (k + 1)]


def take_wide(s, c, width):
    at = pl.ds(pl.multiple_of((c // (SPAN // width)) * D, D), D)
    lanes = pl.ds(pl.multiple_of(lax.rem(c, SPAN // width) * width, width), width)
    return s.sc[0, at, lanes]


def column_cells(s, col, nr):
    local = ROWS // nr
    width = CELLW
    per = width // local

    def part(c, _):
        sl = pl.ds(pl.multiple_of(c * width, width), width)
        o = jnp.concatenate([s.ot[h, 0:HD, sl] for h in range(HEADS)], 0).astype(bf16)
        s.o2[:, sl] = o
        r2 = s.xt[:, sl].astype(f32) + mm(s.wt[OUT2 : OUT2 + D, :], o)
        n, rstd = ln_forward(r2)
        h2 = (n * s.vect[:, 3:4] + s.vect[:, 4:5]).astype(bf16)
        s.h2b[:, sl] = h2
        bias = jnp.concatenate([s.vect[:, 8:9], s.vect[:, 9:10]], 0)
        u = mm(s.wt[UP : UP + FFN, :], h2) + bias
        usq = u * u
        th = jnp.tanh(GELU * u * (1.0 + 0.044715 * usq))
        half = 0.5 * (1.0 + th)
        g = (u * half).astype(bf16)
        slope = half + 0.5 * u * (1.0 - th * th) * (GELU * (1.0 + 0.134145 * usq))
        s.gb[:, sl] = g
        r3 = h2.astype(f32) + mm(s.w[:, DOWN : DOWN + FFN], g) + s.vect[:, 7:8]
        n3, rstd3 = ln_forward(r3)
        out = (n3 * s.vect[:, 5:6] + s.vect[:, 6:7]).astype(bf16)
        for k in range(per):
            s.et[col * nr + c * per + k] = out[:, local * k : local * (k + 1)]
        up = jnp.concatenate([s.gr[c * per + k, col] for k in range(per)], 1).astype(f32)
        s.vacc[5] += fold(up * n3)
        s.vacc[6] += fold(up)
        dr3 = ln_backward(up, n3, rstd3, s.vect[:, 5:6])
        dz = dr3.astype(bf16)
        s.dzb[:, sl] = dz
        s.vacc[7] += fold(dz.astype(f32))
        du = (slope * mm(s.wt[DOWN : DOWN + FFN, :], dz)).astype(bf16)
        s.dub[:, sl] = du
        folded = fold(du.astype(f32))
        s.vacc[8] += folded[0:D]
        s.vacc[9] += folded[D:]
        dh2 = dr3 + mm(s.w[:, UP : UP + FFN], du)
        s.vacc[3] += fold(dh2 * n)
        s.vacc[4] += fold(dh2)
        dr = ln_backward(dh2, n, rstd, s.vect[:, 3:4])
        keep_wide(s, c, width, dr)
        da2 = dr.astype(bf16)
        s.da2b[:, sl] = da2
        do = mm(s.w[:, OUT2 : OUT2 + D], da2).astype(bf16)
        row = iota((16, width), 0)
        for h in range(HEADS):
            recip = s.ot[h, HD : HD + 1, sl]
            scaled = (do[HD * h : HD * (h + 1)].astype(f32) * recip).astype(bf16)
            delta = -jnp.sum(scaled.astype(f32) * s.ot[h, 0:HD, sl], 0, keepdims=True)
            high = delta.astype(bf16).astype(f32)
            tail = jnp.where(row == 0, high, jnp.where(row == 1, delta - high, 0.0))
            base = 64 + HD * (h % 2)
            s.da[h, base : base + HD, sl] = scaled
            s.da[h, 0:16, sl] = tail.astype(bf16)
        return 0

    lax.fori_loop(0, ROWS // width, part, 0)


def column_grads(s):
    s.grads[QKV2 : QKV2 + D, :] += mm_nt(s.dqb[...], s.xt[...])
    s.grads[QKV2 + D : QKV2 + 3 * D, :] += mm_nt(s.dkvb[...], s.xct[...])
    s.grads[UP : UP + FFN, :] += mm_nt(s.dub[...], s.h2b[...])
    s.grads[DOWN : DOWN + FFN, :] += mm_nt(s.gb[...], s.dzb[...])
    s.grads[OUT2 : OUT2 + D, :] += mm_nt(s.da2b[...], s.o2[...])


def column_backward(s):
    def head(h, _):
        mine = pl.ds(pl.multiple_of(HD * h, HD), HD)
        other = pl.ds(pl.multiple_of(D + HD * h, HD), HD)
        t = mm(s.vb[h // 2], s.da[h])
        ds = s.ex[h] * t.astype(bf16)
        s.dqb[mine, :] = (mm(s.kt[mine, :], ds) * SCALE).astype(bf16)
        odd = HD * lax.rem(h, 2)
        do = s.da[h, pl.ds(pl.multiple_of(64 + odd, HD), HD), :]
        q = s.qa[h, pl.ds(pl.multiple_of(odd, HD), HD), :]
        s.dkvb[other, :] = mm_nt(do, s.ex[h]).astype(bf16)
        s.dkvb[mine, :] = (mm_nt(q, ds) * SCALE).astype(bf16)
        return 0

    lax.fori_loop(0, HEADS, head, 0)


def column_finish(s, col, nr, order, done):
    local = ROWS // nr
    width = max(local, CHUNK)
    per = width // local
    s.kt[...] = mm(s.w[:, QKV2 + D : QKV2 + 3 * D], s.dkvb[...]).astype(bf16)

    for c in order:
        sl = pl.ds(pl.multiple_of(c * width, width), width)
        dh = take_wide(s, c, width) + mm(s.w[:, QKV2 : QKV2 + D], s.dqb[:, sl]) + mm_nt(s.kt[...], s.pick[sl, :])
        out = dh.astype(bf16)
        for k in range(per):
            s.hs[col * nr + c * per + k] = out[:, local * k : local * (k + 1)]
        for k in range(per):
            done(c * per + k)


def rows_norm_back(s, f, per):
    local = s.et.shape[2]

    def wide(ref):
        return jnp.concatenate([ref[f + k] for k in range(per)], 1)

    dh = wide(s.dr).astype(f32)
    n = wide(s.n1)
    s.vacc[1] += fold(dh * n)
    s.vacc[2] += fold(dh)
    dr = ln_backward(dh, n, wide(s.rstd1), s.vect[:, 1:2])
    absent = jnp.concatenate([s.missing[pl.ds(f + k, 1), :] for k in range(per)], 1) > 0
    s.vacc[0] += fold(jnp.where(absent, dr, 0.0))
    da = dr.astype(bf16)
    on = jnp.concatenate([s.on[f + k] for k in range(per)], 0).astype(bf16)
    s.grads[OUT1 : OUT1 + D, :] += mm(da, on)
    do = mm_nt(eye(local * per), mm(s.w[:, OUT1 : OUT1 + D], da).astype(bf16))
    for k in range(per):
        at = slice(local * k, local * (k + 1))
        s.n1[f + k] = dr[:, at]
        s.nat[f + k, :, 0:D] = do[at]


def group_main(s, low, high):
    ident = eye(D)

    def start(i, base):
        don = jnp.concatenate([group_cells(s.nat, 2 * i), group_cells(s.nat, 2 * i + 1)], 0)
        do = mm_nt(ident, don[:, 0:D])
        for k in range(2):
            g = 2 * i + k
            for h in range(HEADS):
                hs = slice(HD * h, HD * (h + 1))
                hl = slice(CELLS * h, CELLS * (h + 1))
                scaled = (do[hs, CELLS * k : CELLS * (k + 1)] * s.inv[g, :, hl]).astype(bf16)
                s.dbd[base + k, hs, hl] = scaled
                part = scaled.astype(f32) * s.og1[g, hs, :].astype(f32)
                s.delta[base + k, :, hl] = jnp.sum(part, 0, keepdims=True)

    def rest(i, k, base):
        g = 2 * i + k
        t = mm(s.vn[g], s.dbd[base + k]) - s.delta[base + k]
        exb = s.expo[g]
        ds = (exb.astype(f32) * t).astype(bf16)
        at = slice(CELLS * k, CELLS * (k + 1))
        for h in range(HEADS):
            hs = slice(HD * h, HD * (h + 1))
            ks = slice(D + HD * h, D + HD * (h + 1))
            vs = slice(2 * D + HD * h, 2 * D + HD * (h + 1))
            hl = slice(CELLS * h, CELLS * (h + 1))
            dq = mm(s.qkv[i, ks, at], ds[:, hl]) * SCALE
            dk = mm_nt(s.qkv[i, hs, at], ds[:, hl]) * SCALE
            dv = mm_nt(s.dbd[base + k, hs, hl], exb[:, hl])
            s.qkv[i, hs, at] = dq.astype(bf16)
            s.qkv[i, ks, at] = dk.astype(bf16)
            s.qkv[i, vs, at] = dv.astype(bf16)

    def both(i, base):
        for k in range(2):
            rest(i, k, base)

    def body(j, _):
        i = low + 2 * j
        start(i + 1, 2)
        both(i, 0)
        start(jnp.minimum(i + 2, high - 1), 0)
        both(i + 1, 2)
        return 0

    start(low, 0)
    lax.fori_loop(0, (high - low) // 2, body, 0)


def group_grad(s):
    res = 0.0
    for i in range(s.qkv.shape[0]):
        res = res + mm(s.qkv[i], s.eg[2 * CELLS * i : 2 * CELLS * (i + 1), :])
    s.grads[QKV1 : QKV1 + 3 * D, :] = res[:, 0:D]
    gone = res[:, D:EAUG]
    high = gone.astype(bf16)
    low = (gone - high.astype(f32)).astype(bf16)
    w = s.w[:, QKV1 : QKV1 + 3 * D]
    s.vacc[0, :, 0:16] += mm(w, high) + mm(w, low)


def group_close(s, local):
    pairs = local // SUB // 2

    def close(i, _):
        de = mm(s.w[:, QKV1 : QKV1 + 3 * D], s.qkv[i]).T
        for k in range(2):
            rows = pl.ds(pl.multiple_of((2 * i + k) * SUB, SUB), SUB)
            s.on[:, rows, :] = de[CELLS * k : CELLS * (k + 1)].reshape(F, SUB, D)
        return 0

    lax.fori_loop(0, pairs, close, 0)


def rows_finish(s):
    def one(f, _):
        absent = s.missing[pl.ds(f, 1), :] > 0
        de = s.n1[f] + s.on[f].T
        s.et[f] = jnp.where(absent, 0.0, de).astype(bf16)
        return 0

    lax.fori_loop(0, F, one, 0, unroll=2)


def adam(param, grad, first, second, average, rate):
    first_new = B1 * first + (1.0 - B1) * grad
    second_new = B2 * second + (1.0 - B2) * grad * grad
    first_hat = first_new * (1.0 / (1.0 - B1**STEP))
    second_hat = second_new * (1.0 / (1.0 - B2**STEP))
    param_new = param - rate * (first_hat / (jnp.sqrt(second_hat) + ADAM_EPS) + DECAY * param)
    average_new = EMA * average + (1.0 - EMA) * param_new
    return param_new, first_new, second_new, average_new


def local_scratch(nr):
    local = ROWS // nr
    fc = F // nr
    groups = local // SUB
    return dict(
        wt=((COLS, D), bf16),
        w=((D, COLS), bf16),
        vect=((D, 16), f32),
        et=((F, D, local), bf16),
        nat=((F, local, EAUG), f32),
        on=((F, local, D), f32),
        eg=((groups * CELLS, EAUG), bf16),
        qkv=((groups // 2, 3 * D, 2 * CELLS), bf16),
        vn=((groups, CELLS, D), bf16),
        expo=((groups, CELLS, WIDE), bf16),
        inv=((groups, 1, WIDE), f32),
        og1=((groups, D, CELLS), bf16),
        n1=((F, D, local), f32),
        rstd1=((F, 1, local), f32),
        qbd=((2, GAUG, WIDE), bf16),
        dbd=((4, D, WIDE), bf16),
        delta=((4, 1, WIDE), f32),
        kaug=((2 * groups, CELLS, 128), bf16),
        pick=((ROWS, KEYS), bf16),
        xt=((D, ROWS), bf16),
        xct=((D, KEYS), bf16),
        kt=((D, KEYS), bf16),
        ka=((HEADS // 2, KEYS, 128), bf16),
        vb=((HEADS // 2, KEYS, 128), bf16),
        sc=((2, KEYS, SPAN), f32),
        top=((2, 8, SPAN), f32),
        va=((HEADS, HD + 16, KEYS), bf16),
        qa=((HEADS, KAUG, ROWS), bf16),
        da=((HEADS, 128, ROWS), bf16),
        ex=((HEADS, KEYS, ROWS), bf16),
        ot=((HEADS, HD + 8, ROWS), f32),
        o2=((D, ROWS), bf16),
        h2b=((D, ROWS), bf16),
        gb=((FFN, ROWS), bf16),
        dub=((FFN, ROWS), bf16),
        dzb=((D, ROWS), bf16),
        da2b=((D, ROWS), bf16),
        dqb=((D, ROWS), bf16),
        dkvb=((2 * D, KEYS), bf16),
        vacc=((10, D, 128), f32),
        grads=((COLS + 32, D), f32),
        hs=((F, D, local), bf16),
        hr=((nr, fc, D, local), bf16),
        gr=((nr, fc, D, local), bf16),
        dr=((F, D, local), bf16),
    )


IN_NAMES = ["cells", "missing", "count", "og", "mat", "vec"]
OUT_NAMES = ["layer", "igrad", "norm", "mgrad", "vgrad"]


def shapes_of(width):
    first = -(-(width + 1) // 16) * 16
    half = -(-(-(-(width + 1) // 2)) // 8) * 8
    return first, half, first + -(-half // 16) * 16


def pack(block, width):
    first, half, total = shapes_of(width)
    rows = block.shape[0]
    low = block[:, 0:128]
    if rows < first:
        low = jnp.concatenate([low, jnp.zeros((first - rows, 128), f32)], 0)
    high = block[:, 128:D]
    high = jnp.concatenate([high, jnp.zeros((2 * half - rows, 64), f32)], 0)
    high = jnp.concatenate([high[0:half], high[half:]], 1)
    if half < total - first:
        high = jnp.concatenate([high, jnp.zeros((total - first - half, 128), f32)], 0)
    return jnp.concatenate([low, high], 0)


def unpack(packed, width, rows):
    first, half, total = shapes_of(width)
    low = packed[0:rows]
    high = packed[first : first + half]
    high = jnp.concatenate([high[:, 0:64], high[0 : rows - half, 64:128]], 0)
    return jnp.concatenate([low, high], 1)


def whole_kernel(nr, n, names, *refs):
    s = Refs(names, refs)
    if not hasattr(s, "kaug"):
        s.kaug = s.sib
    local = ROWS // nr
    fc = F // nr
    width = s.mat.shape[0]
    t = lax.axis_index("table")
    row = lax.axis_index("row")
    me = t * nr + row
    core = lax.rem(t, 2)
    nt = n // nr
    nx, nz = nt // 2, 4
    ny = nr // nz
    x, z, y = t // 2, row // ny, lax.rem(row, ny)
    flat = x * ny + y
    plane = nx * ny
    critical = -(-4 * D // width)
    late = -(-3 * D // width)
    sibling = (t + 1 - 2 * core, row)
    barrier = pltpu.get_barrier_semaphore()

    def place(p):
        return (p // nr, lax.rem(p, nr))

    def core_of(p):
        return lax.rem(p // nr, 2)

    def remote(src, dst, send, recv, device):
        return pltpu.make_async_remote_copy(
            src_ref=src, dst_ref=dst, send_sem=send, recv_sem=recv, device_id=device, device_id_type=MESH
        )

    def others(count, first, body):
        def step(k, _):
            body(lax.rem(first + k, count))
            return 0

        lax.fori_loop(1, count, step, 0)

    def along(j):
        return (t, lax.rem(z + j, nz) * ny + y)

    def across(j):
        q = lax.rem(flat + j, plane)
        return (2 * (q // ny) + core, z * ny + lax.rem(q, ny))

    def on_line(p):
        return ((p // nr) == t) & (lax.rem(p, ny) == y)

    def slots(low, high, want, body):
        def step(p, _):
            @pl.when(want(p))
            def _():
                body(p)

            return 0

        lax.fori_loop(low, high, step, 0)

    def mine(p):
        return core_of(p) == core

    def theirs(p):
        return core_of(p) != core

    def mine_not_me(p):
        return (core_of(p) == core) & (p != me)

    def greet(p):
        q = lax.rem(p, nr)

        @pl.when(((p // nr) == t) | (q == row) | ((core_of(p) == core) & ((q // ny) == z)))
        def _():
            pl.semaphore_signal(barrier, inc=1, device_id=place(p), device_id_type=MESH)

    others(n, me, greet)
    partners = (nr - 1) + (nt - 1) + (nx - 1) * (ny - 1)

    stage = pltpu.make_async_copy(s.cells, s.hs, s.c_sem)
    stage.start()
    s.wr[me] = pack(s.mat[...], width).astype(bf16)
    v = jnp.concatenate([s.vec[...], jnp.zeros((128 - 10, D), f32)], 0)
    v = jnp.concatenate([v, jnp.zeros((128, 256 - D), f32)], 1).T
    s.vect[...] = v[0:D, 0:16]
    pl.semaphore_wait(barrier, partners)

    def weights(slot, send, device):
        return remote(s.wr.at[slot], s.wr.at[slot], send, s.w_recv.at[slot], device)

    def by_line(j):
        return weights(me, s.wz_send.at[j], along(j))

    def by_plane(slot, j):
        return weights(slot, s.wp_send.at[slot, j], across(j))

    def by_core(slot):
        return weights(slot, s.wc_send.at[slot], sibling)

    def arrive(slot):
        weights(slot, s.wc_send.at[slot], sibling).wait_recv()

    def line_slot(j):
        return t * nr + lax.rem(z + j, nz) * ny + y

    def to_all(slot):
        for j in range(1, plane):
            by_plane(slot, j).start()
        by_core(slot).start()

    def line_arrivals(want):
        for j in range(1, nz):
            p = line_slot(j)

            @pl.when(want(p))
            def _(p=p):
                arrive(p)
                to_all(p)

    def plane_arrivals(want):
        def step(i, _):
            q = lax.rem(flat + 1 + i // nz, plane)
            p = (2 * (q // ny) + core) * nr + lax.rem(i, nz) * ny + lax.rem(q, ny)

            @pl.when(want(p))
            def _():
                arrive(p)
                by_core(p).start()

            return 0

        lax.fori_loop(0, (plane - 1) * nz, step, 0)

    def is_critical(p):
        return p < critical

    def is_other(p):
        return p >= critical

    order = [lax.rem(z + 2, nz), 3 - z, z + 1 - 2 * lax.rem(z, 2), z]

    def peers(body):
        for zz in order:
            for yy in range(ny):
                p = zz * ny + yy

                @pl.when(p != row)
                def _(p=p):
                    body(p)

    def unpack_slots(low, high):
        for p in range(low, high):
            s.grads[p * width : (p + 1) * width, :] = unpack(s.wr[p].astype(f32), width, width)

    def spread(low, high):
        for k in range(low // 128, high // 128):
            piece = s.grads[128 * k : 128 * (k + 1), :]
            s.wt[128 * k : 128 * (k + 1), :] = piece.astype(bf16)
            s.w[:, 128 * k : 128 * (k + 1)] = piece.T.astype(bf16)

    def give_grad(p, col):
        return remote(
            s.og.at[col * nr + p], s.gr.at[row, col], s.g_send.at[col, p], s.g_recv.at[col, row], (t, p)
        )

    def got_grad(p, col):
        return remote(
            s.og.at[col * nr + p], s.gr.at[p, col], s.g_send.at[col, p], s.g_recv.at[col, p], (t, p)
        )

    def publish():
        for j in range(1, nz):
            by_line(j).start()
        to_all(me)

    publish()
    stage.wait()
    embed(s, local)
    line_arrivals(is_critical)
    group_setup(s)
    s.vacc[...] = jnp.zeros(s.vacc.shape, f32)
    plane_arrivals(is_critical)

    line_arrivals(is_other)

    peers(lambda p: give_grad(p, 0).start())
    slots(0, critical, theirs, arrive)
    unpack_slots(0, critical)
    spread(0, 4 * D)

    group_forward(s, local)

    def give(p, col):
        return remote(
            s.hs.at[col * nr + p], s.hr.at[row, col], s.h_send.at[col, p], s.h_recv.at[col, row], (t, p)
        )

    def got(p, col):
        return remote(
            s.hs.at[col * nr + p], s.hr.at[p, col], s.h_send.at[col, p], s.h_recv.at[col, p], (t, p)
        )

    for col in range(fc):
        for zz in order:
            rows_norm(s, col * nr + zz * ny, ny)
            for yy in range(ny):
                q = zz * ny + yy

                @pl.when(q != row)
                def _(q=q, col=col):
                    give(q, col).start()

        s.hr[row, col] = s.hs[col * nr + row]
    for col in range(1, fc):
        peers(lambda p, col=col: give_grad(p, col).start())
    own = [pltpu.make_async_copy(s.og.at[col * nr + row], s.gr.at[row, col], s.o_sem.at[col]) for col in range(fc)]
    for c in own:
        c.start()
    for c in own:
        c.wait()
    plane_arrivals(is_other)
    make_pick(s)
    s.da[...] = jnp.zeros(s.da.shape, bf16)
    slots(critical, n, theirs, arrive)
    unpack_slots(critical, n)
    spread(4 * D, COLS)
    s.grads[...] = jnp.zeros(s.grads.shape, f32)

    def back_layer(p, col):
        return remote(
            s.et.at[col * nr + p], s.layer.at[col * nr + row], s.l_send.at[col, p], s.l_recv.at[col * nr + row], (t, p)
        )

    def back_grad(p, col):
        return remote(
            s.hs.at[col * nr + p], s.dr.at[col * nr + row], s.d_send.at[col, p], s.d_recv.at[col * nr + row], (t, p)
        )

    def sent_rows(p):
        for c in range(fc):
            give(p, c).wait_send()

    def keep(col):
        return pltpu.make_async_copy(s.et.at[col * nr + row], s.layer.at[col * nr + row], s.k_sem.at[col])

    for col in range(fc):
        others(nr, row, lambda p: got(p, col).wait_recv())
        column_project(s, col, nr)
        column_forward(s)
        others(nr, row, lambda p: got_grad(p, col).wait_recv())
        column_cells(s, col, nr)
        peers(lambda p, col=col: back_layer(p, col).start())
        keep(col).start()
        column_backward(s)
        if col == 0:
            peers(sent_rows)

        def finished(p, col=col):
            @pl.when(p != row)
            def _():
                back_grad(p, col).start()

        column_finish(s, col, nr, order, finished)
        column_grads(s)
        s.dr[col * nr + row] = s.hs[col * nr + row]

    def totals(v):
        if v >= 10:
            return None
        acc = s.vacc[v]
        high = acc.astype(bf16)
        low = (acc - high.astype(f32)).astype(bf16)
        ones = jnp.ones((16, 128), bf16)
        return (mm_nt(ones, high) + mm_nt(ones, low))[0:1]

    def piece(p, extra=None):
        block = s.grads[p * width : (p + 1) * width, :]
        last = jnp.zeros((8, D), f32) if extra is None else jnp.broadcast_to(extra, (8, D))
        last = jnp.where(iota((8, D), 0) == 0, last, 0.0)
        s.wr[p] = pack(jnp.concatenate([block, last], 0)[0 : width + 1], width).astype(bf16)

    def exchange(p):
        return remote(s.wr.at[p], s.sib.at[p], s.x_send.at[p], s.x_recv.at[p], sibling)

    def inward(p, j, k):
        return remote(s.sib.at[p], s.pin.at[j, k], s.p_send.at[p], s.p_recv.at[j, k], across(j))

    def outward(j):
        k = lax.rem(z + j, nz)
        return remote(s.two.at[k], s.zin.at[j], s.z_send.at[j], s.z_recv.at[j], along(j))

    def steps_to(p):
        q = (p // nr // 2) * ny + lax.rem(p, ny)
        return lax.rem(q - flat + plane, plane)

    def z_of(p):
        return lax.rem(p, nr) // ny

    def to_sibling(low, high):
        slots(low, high, theirs, lambda p: exchange(p).start())

    def to_plane(low, high):
        def send(p):
            exchange(p).wait_recv()
            s.sib[p] = (s.wr[p].astype(f32) + s.sib[p].astype(f32)).astype(bf16)

            @pl.when(jnp.logical_not(on_line(p)))
            def _():
                inward(p, steps_to(p), z_of(p)).start()

        slots(low, high, mine, send)

    def to_line(low, high):
        def send(p):
            k = z_of(p)
            total = s.sib[p].astype(f32)
            for j in range(1, plane):
                inward(p, j, k).wait_recv()
                total = total + s.pin[j, k].astype(f32)
            s.two[k] = total.astype(bf16)

            @pl.when(p != me)
            def _():
                outward(lax.rem(k - z + nz, nz)).start()

        slots(low, high, on_line, send)

    def tell(src, p):
        return remote(s.note, s.notes.at[src], s.n_send.at[p], s.n_recv.at[src], (t, p))

    def share(j):
        tt = lax.rem(t + j, nt)
        own = s.notes.at[pl.ds(t * nr, nr)]
        return remote(own, own, s.s_send.at[j], s.s_recv.at[t], (tt, row))

    def shared(j):
        tt = lax.rem(t + j, nt)
        other = s.notes.at[pl.ds(tt * nr, nr)]
        return remote(other, other, s.s_send.at[j], s.s_recv.at[tt], (tt, row))

    def spread_notes():
        others(nr, row, lambda p: tell(t * nr + p, p).wait_recv())
        for j in range(1, nt):
            share(j).start()

    def settle():
        total = s.two[z].astype(f32)
        for j in range(1, nz):
            outward(j).wait_recv()
            total = total + s.zin[j].astype(f32)
        total = unpack(total, width, width + 1)
        vec_row = total[width : width + 1, :]
        grad = total[0:width]
        s.mgrad[...] = grad
        squares = jnp.sum(jnp.sum(grad * grad, 0, keepdims=True), 1, keepdims=True)
        tail = jnp.concatenate([vec_row[:, 128:D], jnp.broadcast_to(squares, (1, 64))], 1)
        s.note[...] = jnp.concatenate([vec_row[:, 0:128], tail], 0)
        s.notes[me] = s.note[...]
        peers(lambda p: tell(me, p).start())

    for j in range(1, nz):
        by_line(j).wait_send()

    def left(p):
        by_core(p).wait_send()

        @pl.when(on_line(p))
        def _():
            for j in range(1, plane):
                by_plane(p, j).wait_send()

    slots(0, n, mine, left)
    for p in range(critical, n):
        piece(p, totals(p))
    to_sibling(critical, n)

    for col in range(fc):
        if col == fc - 1:
            to_plane(critical, n)
        for zz in order[::-1]:
            for yy in range(ny):
                q = zz * ny + yy

                @pl.when(q != row)
                def _(q=q, col=col):
                    f = col * nr + q
                    remote(s.hs.at[f], s.dr.at[f], s.d_send.at[col, q], s.d_recv.at[f], (t, q)).wait_recv()

            rows_norm_back(s, col * nr + zz * ny, ny)
    for p in range(late, critical):
        piece(p, totals(p))
    to_sibling(late, critical)
    pairs = local // SUB // 2
    group_main(s, 0, pairs // 2)
    to_line(critical, n)
    to_plane(late, critical)
    group_main(s, pairs // 2, pairs)
    to_line(late, critical)
    group_grad(s)
    for p in range(late):
        piece(p, totals(p))
    to_sibling(0, late)

    first_early = -(-late // nr)

    @pl.when(t >= first_early)
    def _():
        settle()

    group_close(s, local)
    to_plane(0, late)

    @pl.when(t >= first_early)
    def _():
        spread_notes()

    for col in range(fc):
        peers(lambda p, col=col: back_layer(p, col).wait_send())
        keep(col).wait()
    rows_finish(s)
    result = pltpu.make_async_copy(s.et, s.igrad, s.c_sem)
    result.start()
    to_line(0, late)

    @pl.when(t < first_early)
    def _():
        settle()
        spread_notes()

    for j in range(1, nt):
        shared(j).wait_recv()
    squares = lax.fori_loop(0, n, lambda k, x: x + s.notes[k, 1:2, 64:65], jnp.zeros((1, 1), f32))
    vec_total = jnp.concatenate(
        [jnp.concatenate([s.notes[p, 0:1, :], s.notes[p, 1:2, 0:64]], 1) for p in range(10)], 0
    )
    squares = squares + jnp.sum(jnp.sum(vec_total * vec_total, 0, keepdims=True), 1, keepdims=True)
    norm = jnp.sqrt(squares)
    s.norm[...] = norm
    factor = CLIP / jnp.maximum(norm, CLIP)
    s.mgrad[...] = s.mgrad[...] * factor
    s.vgrad[...] = vec_total * factor

    result.wait()
    for j in range(1, nz):
        outward(j).wait_send()

    def departed(p):
        @pl.when(jnp.logical_not(on_line(p)))
        def _():
            inward(p, steps_to(p), z_of(p)).wait_send()

    slots(0, n, mine, departed)
    slots(0, n, theirs, lambda p: exchange(p).wait_send())
    peers(lambda p: tell(me, p).wait_send())
    for j in range(1, nt):
        share(j).wait_send()

    def sent_row(p):
        for col in range(fc):
            give_grad(p, col).wait_send()
            back_grad(p, col).wait_send()
            f = col * nr + p
            remote(s.et.at[col * nr + p], s.layer.at[f], s.l_send.at[col, p], s.l_recv.at[f], (t, p)).wait_recv()

    others(nr, row, sent_row)


def update_kernel(*refs):
    ins, outs = refs[0:12], refs[13:23]
    refs[23][...] = refs[12][...]
    held, made = refs[24:36], refs[36:44]
    in_sem, out_sem = refs[44:46]
    loads = [pltpu.make_async_copy(a, b, in_sem.at[k]) for k, (a, b) in enumerate(zip(ins, held))]
    sources = held[0:2] + made
    stores = [pltpu.make_async_copy(a, b, out_sem.at[k]) for k, (a, b) in enumerate(zip(sources, outs))]
    for load in loads[2:] + loads[:2]:
        load.start()
    for load in loads[2:]:
        load.wait()
    w, grad, m1, m2, m3, v, vgrad, v1, v2, v3 = (ref[...] for ref in held[2:12])
    for k, value in enumerate(adam(w, grad, m1, m2, m3, RATE) + adam(v, vgrad, v1, v2, v3, VEC_RATE)):
        made[k][...] = value
        stores[k + 2].start()
    for load, store in zip(loads[:2], stores[:2]):
        load.wait()
        store.start()
    for store in stores:
        store.wait()


def on_device(nr, n, cells, missing, train_counts, out_grad, matrices, vectors, m1, m2, m3, v1, v2, v3):
    local = ROWS // nr
    fc = F // nr
    width = matrices.shape[1]
    packed = (shapes_of(width)[2], 128)
    plane = n // 2 // 4
    sds = jax.ShapeDtypeStruct
    big = sds((F, D, local), bf16)
    dma = pltpu.SemaphoreType.DMA
    scratch = {k: pltpu.VMEM(shape, dtype) for k, (shape, dtype) in local_scratch(nr).items()}
    scratch.update(
        wr=pltpu.VMEM((n,) + packed, bf16),
        sib=pltpu.VMEM((n,) + packed, bf16),
        pin=pltpu.VMEM((plane, 4) + packed, bf16),
        two=pltpu.VMEM((4,) + packed, bf16),
        zin=pltpu.VMEM((4,) + packed, bf16),
        note=pltpu.VMEM((2, 128), f32),
        notes=pltpu.VMEM((n, 2, 128), f32),
        w_recv=dma((n,)),
        c_sem=dma(()),
        o_sem=dma((fc,)),
        k_sem=dma((fc,)),
        wz_send=dma((4,)),
        wp_send=dma((n, plane)),
        wc_send=dma((n,)),
        h_send=dma((fc, nr)),
        h_recv=dma((fc, nr)),
        g_send=dma((fc, nr)),
        g_recv=dma((fc, nr)),
        l_send=dma((fc, nr)),
        l_recv=dma((F,)),
        d_send=dma((fc, nr)),
        d_recv=dma((F,)),
        x_send=dma((n,)),
        x_recv=dma((n,)),
        p_send=dma((n,)),
        p_recv=dma((plane, 4)),
        z_send=dma((4,)),
        z_recv=dma((4,)),
        n_send=dma((nr,)),
        n_recv=dma((n,)),
        s_send=dma((n // nr,)),
        s_recv=dma((n // nr,)),
    )
    shared = scratch["sib"].shape == scratch["kaug"].shape
    if shared:
        del scratch["kaug"]
    names = IN_NAMES + OUT_NAMES + list(scratch)
    in_specs = [VMEM] * 6
    in_specs[0] = in_specs[3] = pl.BlockSpec(memory_space=pl.ANY)
    in_specs[2] = pl.BlockSpec(memory_space=pltpu.SMEM)
    layer, igrad, norm, mgrad, vgrad = pl.pallas_call(
        functools.partial(whole_kernel, nr, n, names),
        out_shape=[big, big, sds((1, 1), f32), sds((width, D), f32), sds((10, D), f32)],
        in_specs=in_specs,
        out_specs=[pl.BlockSpec(memory_space=pl.ANY)] * 2 + [VMEM] * 3,
        scratch_shapes=list(scratch.values()),
        name="whole",
        compiler_params=pltpu.CompilerParams(
            collective_id=0, has_side_effects=True, vmem_limit_bytes=63 * 2**20
        ),
    )(
        cells[0].transpose(1, 2, 0),
        missing[0].T,
        train_counts,
        out_grad[0].transpose(1, 2, 0),
        matrices.T,
        vectors,
    )
    mat = sds((width, D), f32)
    vec = sds((10, D), f32)
    anywhere = pl.BlockSpec(memory_space=pl.ANY)
    held = [big] * 2 + [mat] * 5 + [vec] * 5
    made = [mat] * 4 + [vec] * 4
    layer, igrad, *rest, norm = pl.pallas_call(
        update_kernel,
        out_shape=[big, big] + made + [sds((1, 1), f32)],
        in_specs=[anywhere] * 12 + [VMEM],
        out_specs=[anywhere] * 10 + [VMEM],
        scratch_shapes=[pltpu.VMEM(x.shape, x.dtype) for x in held + made] + [dma((12,)), dma((10,))],
        name="update",
    )(layer, igrad, matrices.T, mgrad, m1.T, m2.T, m3.T, vectors, vgrad, v1, v2, v3, norm)
    back = (2, 0, 1)
    return (
        layer.transpose(back)[None],
        igrad.transpose(back)[None],
        norm[0, 0],
        *[m.T for m in rest[:4]],
        *rest[4:],
    )


def solution(mesh):
    rows = P("table", "row", None, None)
    shard = P(None, ("table", "row"))
    nr = mesh.shape["row"]
    return jax.shard_map(
        functools.partial(on_device, nr, nr * mesh.shape["table"]),
        mesh=mesh,
        in_specs=(rows, P("table", "row", None), P("table"), rows, shard, P(), shard, shard, shard, P(), P(), P()),
        out_specs=(rows, rows, P(), shard, shard, shard, shard, P(), P(), P(), P()),
        check_vma=False,
    )
```

```python
import functools
import math

import jax
import jax.numpy as jnp
from jax import lax
from jax.experimental import pallas as pl
from jax.experimental.pallas import tpu as pltpu
from jax.sharding import PartitionSpec as P

D = 192
FFN = 384
HEADS = 6
HD = 32
ROWS = 1024
F = 16
STEP = 10
KEYS = ROWS * 3 // 4
COLS = 8 * D + 2 * FFN
SUB = 8
CELLS = SUB * F
WIDE = CELLS * HEADS
GAUG = D + 16
EAUG = D + 16
KAUG = 80
CHUNK = 256
SPAN = 512
CELLW = 1024

EPS = 1e-05
MIXER = 37
CLIP = 1.0
RATE = 0.1
VEC_RATE = 0.5
B1 = 0.9
B2 = 0.99
ADAM_EPS = 1e-08
DECAY = 0.01
EMA = 0.9
SCALE = HD ** (-0.5)
EXPC = SCALE * math.log2(math.e)
NEG = -1e30
GELU = math.sqrt(2.0 / math.pi)

QKV1, OUT1, QKV2, OUT2, UP, DOWN = 0, 3 * D, 4 * D, 7 * D, 8 * D, 8 * D + FFN

bf16 = jnp.bfloat16
f32 = jnp.float32
MESH = pl.DeviceIdType.MESH
VMEM = pl.BlockSpec(memory_space=pltpu.VMEM)
NT_DIMS = (((1,), (1,)), ((), ()))


def mm(a, b):
    return jnp.dot(a, b, preferred_element_type=f32)


def mm_nt(a, b):
    return lax.dot_general(a, b, NT_DIMS, preferred_element_type=f32)


def iota(shape, dim):
    return lax.broadcasted_iota(jnp.int32, shape, dim)


def eye(size):
    return (iota((size, size), 0) == iota((size, size), 1)).astype(bf16)


def ln_forward(r):
    center = r - jnp.sum(r, 0, keepdims=True) * (1.0 / D)
    spread = jnp.sum(center * center, 0, keepdims=True) * (1.0 / D)
    rstd = lax.rsqrt(spread + EPS)
    return center * rstd, rstd


def ln_backward(dy, n, rstd, gain):
    dn = dy * gain
    mean_one = jnp.sum(dn, 0, keepdims=True) * (1.0 / D)
    mean_two = jnp.sum(dn * n, 0, keepdims=True) * (1.0 / D)
    return (dn - mean_one - n * mean_two) * rstd


def fold(x):
    total = x[:, 0:128]
    for k in range(1, x.shape[1] // 128):
        total = total + x[:, 128 * k : 128 * (k + 1)]
    return total


def fit(x):
    if x.shape[1] >= 128:
        return fold(x)
    return jnp.concatenate([x, jnp.zeros((x.shape[0], 128 - x.shape[1]), x.dtype)], 1)


class Refs:
    def __init__(self, names, refs):
        for name, ref in zip(names, refs, strict=True):
            setattr(self, name, ref)


def embed(s, local):
    ident = eye(local)
    shade = s.vect[:, 0:1]

    def one(f, _):
        absent = s.missing[pl.ds(f, 1), :] > 0
        e = jnp.where(absent, shade, s.hs[f].astype(f32)).astype(bf16)
        s.et[f] = e
        flag = jnp.where((iota((16, local), 0) == 0) & absent, 1.0, 0.0).astype(bf16)
        s.nat[f] = mm_nt(ident, jnp.concatenate([e, flag], 0))
        return 0

    lax.fori_loop(0, F, one, 0, unroll=2)


def group_setup(s):
    same = jnp.where((iota((16, WIDE), 1) % SUB) == iota((16, WIDE), 0), 0.0, NEG).astype(bf16)
    hot = (iota((CELLS, 16), 0) % SUB == iota((CELLS, 16), 1)).astype(bf16)
    for k in range(2):
        s.qbd[k, 0:D, :] = jnp.zeros((D, WIDE), bf16)
        s.qbd[k, D:GAUG, :] = same
        s.dbd[k] = jnp.zeros((D, WIDE), bf16)
        s.dbd[k + 2] = jnp.zeros((D, WIDE), bf16)
    for g in range(s.vn.shape[0]):
        s.kaug[2 * g + 1, :, 64:80] = hot


def group_cells(ref, g):
    at = pl.ds(pl.multiple_of(g * SUB, SUB), SUB)
    return ref[:, at, :].reshape(CELLS, EAUG).astype(bf16)


def group_forward(s, local):
    ident = eye(CELLS)
    pairs = local // SUB // 2

    def project(i):
        eg = jnp.concatenate([group_cells(s.nat, 2 * i), group_cells(s.nat, 2 * i + 1)], 0)
        s.eg[pl.ds(pl.multiple_of(i * 2 * CELLS, 2 * CELLS), 2 * CELLS), :] = eg
        eg = eg[:, 0:D]
        proj = mm_nt(s.wt[QKV1 : QKV1 + 3 * D, :], eg).astype(bf16)
        kn = mm(eg, s.w[:, QKV1 + D : QKV1 + 3 * D]).astype(bf16)
        s.qkv[i] = proj
        for k in range(2):
            key = kn[CELLS * k : CELLS * (k + 1)]
            s.kaug[4 * i + 2 * k] = key[:, 0:128]
            s.kaug[4 * i + 2 * k + 1, :, 0:64] = key[:, 128:D]
            s.vn[2 * i + k] = kn[CELLS * k : CELLS * (k + 1), D:]

    def score(i, k):
        g = 2 * i + k
        at = slice(CELLS * k, CELLS * (k + 1))
        for h in range(HEADS):
            s.qbd[k, HD * h : HD * (h + 1), CELLS * h : CELLS * (h + 1)] = s.qkv[i, HD * h : HD * (h + 1), at]
        keys = jnp.concatenate([s.kaug[2 * g], s.kaug[2 * g + 1, :, 0:80]], 1)
        scores = mm(keys, s.qbd[k])
        top = jnp.max(scores, 0, keepdims=True)
        ex = jnp.exp2((scores - top) * EXPC)
        s.inv[g] = 1.0 / jnp.sum(ex, 0, keepdims=True)
        s.expo[g] = ex.astype(bf16)

    def result(i, k):
        g = 2 * i + k
        at = slice(CELLS * k, CELLS * (k + 1))
        heads = []
        for h in range(HEADS):
            hl = slice(CELLS * h, CELLS * (h + 1))
            value = s.qkv[i, 2 * D + HD * h : 2 * D + HD * (h + 1), at]
            heads.append(mm(value, s.expo[g, :, hl]) * s.inv[g, :, hl])
        o = jnp.concatenate(heads, 0).astype(bf16)
        s.og1[g] = o
        s.on[:, pl.ds(pl.multiple_of(g * SUB, SUB), SUB), :] = mm_nt(ident, o).reshape(F, SUB, D)

    def body(i, _):
        for k in range(2):
            result(i - 1, k)
        for k in range(2):
            score(i, k)
        project(i + 1)
        return 0

    project(0)
    for k in range(2):
        score(0, k)
    project(1)
    lax.fori_loop(1, pairs - 1, body, 0)
    for k in range(2):
        result(pairs - 2, k)
    for k in range(2):
        score(pairs - 1, k)
    for k in range(2):
        result(pairs - 1, k)


def rows_norm(s, f, per):
    local = s.et.shape[2]
    on = jnp.concatenate([s.on[f + k] for k in range(per)], 0).astype(bf16)
    e = jnp.concatenate([s.et[f + k] for k in range(per)], 1)
    r = e.astype(f32) + mm_nt(s.wt[OUT1 : OUT1 + D, :], on)
    n, rstd = ln_forward(r)
    h = (n * s.vect[:, 1:2] + s.vect[:, 2:3]).astype(bf16)
    for k in range(per):
        at = slice(local * k, local * (k + 1))
        s.n1[f + k] = n[:, at]
        s.rstd1[f + k] = rstd[:, at]
        s.hs[f + k] = h[:, at]


def make_pick(s):
    for c in range(ROWS // 128):
        slot = ((iota((128, KEYS), 0) + 128 * c) * MIXER) % ROWS
        s.pick[128 * c : 128 * (c + 1), :] = (slot == iota((128, KEYS), 1)).astype(bf16)


def column_project(s, col, nr):
    local = ROWS // nr
    count = s.count[0]
    for r in range(nr):
        s.xt[:, local * r : local * (r + 1)] = s.hr[r, col]
    s.xct[...] = mm(s.xt[...], s.pick[...]).astype(bf16)
    kvt = mm(s.wt[QKV2 + D : QKV2 + 3 * D, :], s.xct[...]).astype(bf16)
    s.kt[...] = kvt[0:D]
    q = mm(s.wt[QKV2 : QKV2 + D, :], s.xt[...]).astype(bf16)
    ident = eye(256)
    lane = iota((256, 128), 1)
    ones_v = jnp.where((lane == 0) | (lane == 1), 1.0, 0.0)
    first = jnp.where(iota((16, ROWS), 0) == 0, 1.0, 0.0).astype(bf16)
    for pair in range(HEADS // 2):
        h = 2 * pair
        stack = jnp.concatenate(
            [kvt[part + HD * k : part + HD * (k + 1)] for part in (0, D) for k in (h, h + 1)], 0
        )
        for c in range(KEYS // 256):
            at = slice(256 * c, 256 * (c + 1))
            both = mm_nt(ident, stack[:, at])
            bias = jnp.where((lane == 64) & (iota((256, 128), 0) + 256 * c >= count), NEG, 0.0)
            s.ka[pair, at, :] = jnp.where(lane < 64, both, bias).astype(bf16)
            s.vb[pair, at, :] = jnp.where(lane >= 64, both, ones_v).astype(bf16)
        for k in range(2):
            s.qa[h + k, 0:64, :] = jnp.zeros((64, ROWS), bf16)
            s.qa[h + k, HD * k : HD * (k + 1), :] = q[HD * (h + k) : HD * (h + k + 1), :]
            s.qa[h + k, 64:KAUG, :] = first
            s.va[h + k, 0:HD, :] = kvt[D + HD * (h + k) : D + HD * (h + k + 1)]
            s.va[h + k, HD : HD + 16, :] = jnp.ones((16, KEYS), bf16)


def column_forward(s):
    per = ROWS // SPAN
    steps = HEADS * per

    def place(i):
        return i // per, pl.ds(pl.multiple_of(lax.rem(i, per) * SPAN, SPAN), SPAN)

    def score(i, k):
        h, sl = place(i)
        sc = mm(s.ka[h // 2, :, 0:KAUG], s.qa[h, :, sl])
        s.sc[k] = sc
        s.top[k] = jnp.broadcast_to(jnp.max(sc, 0, keepdims=True), (8, SPAN))

    def weigh(i, k):
        h, sl = place(i)
        ex = jnp.exp2((s.sc[k] - s.top[k, 0:1]) * EXPC).astype(bf16)
        s.ex[h, :, sl] = ex
        o = mm(s.va[h], ex)
        recip = 1.0 / o[HD : HD + 1]
        s.ot[h, 0:HD, sl] = o[0:HD] * recip
        s.ot[h, HD : HD + 8, sl] = jnp.broadcast_to(recip, (8, SPAN))

    def body(i, _):
        score(2 * i + 1, 1)
        weigh(2 * i, 0)
        score(2 * i + 2, 0)
        weigh(2 * i + 1, 1)
        return 0

    score(0, 0)
    lax.fori_loop(0, steps // 2 - 1, body, 0)
    score(steps - 1, 1)
    weigh(steps - 2, 0)
    weigh(steps - 1, 1)


def keep_wide(s, c, width, value):
    for k in range(width // SPAN):
        s.sc[0, D * k : D * (k + 1), :] = value[:, SPAN * k : SPAN * (k + 1)]


def take_wide(s, c, width):
    at = pl.ds(pl.multiple_of((c // (SPAN // width)) * D, D), D)
    lanes = pl.ds(pl.multiple_of(lax.rem(c, SPAN // width) * width, width), width)
    return s.sc[0, at, lanes]


def column_cells(s, col, nr):
    local = ROWS // nr
    width = CELLW
    per = width // local

    def part(c, _):
        sl = pl.ds(pl.multiple_of(c * width, width), width)
        o = jnp.concatenate([s.ot[h, 0:HD, sl] for h in range(HEADS)], 0).astype(bf16)
        s.o2[:, sl] = o
        r2 = s.xt[:, sl].astype(f32) + mm(s.wt[OUT2 : OUT2 + D, :], o)
        n, rstd = ln_forward(r2)
        h2 = (n * s.vect[:, 3:4] + s.vect[:, 4:5]).astype(bf16)
        s.h2b[:, sl] = h2
        bias = jnp.concatenate([s.vect[:, 8:9], s.vect[:, 9:10]], 0)
        u = mm(s.wt[UP : UP + FFN, :], h2) + bias
        usq = u * u
        th = jnp.tanh(GELU * u * (1.0 + 0.044715 * usq))
        half = 0.5 * (1.0 + th)
        g = (u * half).astype(bf16)
        slope = half + 0.5 * u * (1.0 - th * th) * (GELU * (1.0 + 0.134145 * usq))
        s.gb[:, sl] = g
        r3 = h2.astype(f32) + mm(s.w[:, DOWN : DOWN + FFN], g) + s.vect[:, 7:8]
        n3, rstd3 = ln_forward(r3)
        out = (n3 * s.vect[:, 5:6] + s.vect[:, 6:7]).astype(bf16)
        for k in range(per):
            s.et[col * nr + c * per + k] = out[:, local * k : local * (k + 1)]
        up = jnp.concatenate([s.gr[c * per + k, col] for k in range(per)], 1).astype(f32)
        s.vacc[5] += fold(up * n3)
        s.vacc[6] += fold(up)
        dr3 = ln_backward(up, n3, rstd3, s.vect[:, 5:6])
        dz = dr3.astype(bf16)
        s.dzb[:, sl] = dz
        s.vacc[7] += fold(dz.astype(f32))
        du = (slope * mm(s.wt[DOWN : DOWN + FFN, :], dz)).astype(bf16)
        s.dub[:, sl] = du
        folded = fold(du.astype(f32))
        s.vacc[8] += folded[0:D]
        s.vacc[9] += folded[D:]
        dh2 = dr3 + mm(s.w[:, UP : UP + FFN], du)
        s.vacc[3] += fold(dh2 * n)
        s.vacc[4] += fold(dh2)
        dr = ln_backward(dh2, n, rstd, s.vect[:, 3:4])
        keep_wide(s, c, width, dr)
        da2 = dr.astype(bf16)
        s.da2b[:, sl] = da2
        do = mm(s.w[:, OUT2 : OUT2 + D], da2).astype(bf16)
        row = iota((16, width), 0)
        for h in range(HEADS):
            recip = s.ot[h, HD : HD + 1, sl]
            scaled = (do[HD * h : HD * (h + 1)].astype(f32) * recip).astype(bf16)
            delta = -jnp.sum(scaled.astype(f32) * s.ot[h, 0:HD, sl], 0, keepdims=True)
            high = delta.astype(bf16).astype(f32)
            tail = jnp.where(row == 0, high, jnp.where(row == 1, delta - high, 0.0))
            base = 64 + HD * (h % 2)
            s.da[h, base : base + HD, sl] = scaled
            s.da[h, 0:16, sl] = tail.astype(bf16)
        return 0

    lax.fori_loop(0, ROWS // width, part, 0)


def column_grads(s):
    s.grads[QKV2 : QKV2 + D, :] += mm_nt(s.dqb[...], s.xt[...])
    s.grads[QKV2 + D : QKV2 + 3 * D, :] += mm_nt(s.dkvb[...], s.xct[...])
    s.grads[UP : UP + FFN, :] += mm_nt(s.dub[...], s.h2b[...])
    s.grads[DOWN : DOWN + FFN, :] += mm_nt(s.gb[...], s.dzb[...])
    s.grads[OUT2 : OUT2 + D, :] += mm_nt(s.da2b[...], s.o2[...])


def column_backward(s):
    def head(h, _):
        mine = pl.ds(pl.multiple_of(HD * h, HD), HD)
        other = pl.ds(pl.multiple_of(D + HD * h, HD), HD)
        t = mm(s.vb[h // 2], s.da[h])
        ds = s.ex[h] * t.astype(bf16)
        s.dqb[mine, :] = (mm(s.kt[mine, :], ds) * SCALE).astype(bf16)
        odd = HD * lax.rem(h, 2)
        do = s.da[h, pl.ds(pl.multiple_of(64 + odd, HD), HD), :]
        q = s.qa[h, pl.ds(pl.multiple_of(odd, HD), HD), :]
        s.dkvb[other, :] = mm_nt(do, s.ex[h]).astype(bf16)
        s.dkvb[mine, :] = (mm_nt(q, ds) * SCALE).astype(bf16)
        return 0

    lax.fori_loop(0, HEADS, head, 0)


def column_finish(s, col, nr, order, done):
    local = ROWS // nr
    width = max(local, CHUNK)
    per = width // local
    s.kt[...] = mm(s.w[:, QKV2 + D : QKV2 + 3 * D], s.dkvb[...]).astype(bf16)

    for c in order:
        sl = pl.ds(pl.multiple_of(c * width, width), width)
        dh = take_wide(s, c, width) + mm(s.w[:, QKV2 : QKV2 + D], s.dqb[:, sl]) + mm_nt(s.kt[...], s.pick[sl, :])
        out = dh.astype(bf16)
        for k in range(per):
            s.hs[col * nr + c * per + k] = out[:, local * k : local * (k + 1)]
        for k in range(per):
            done(c * per + k)


def rows_norm_back(s, f, per):
    local = s.et.shape[2]

    def wide(ref):
        return jnp.concatenate([ref[f + k] for k in range(per)], 1)

    dh = wide(s.dr).astype(f32)
    n = wide(s.n1)
    s.vacc[1] += fold(dh * n)
    s.vacc[2] += fold(dh)
    dr = ln_backward(dh, n, wide(s.rstd1), s.vect[:, 1:2])
    absent = jnp.concatenate([s.missing[pl.ds(f + k, 1), :] for k in range(per)], 1) > 0
    s.vacc[0] += fold(jnp.where(absent, dr, 0.0))
    da = dr.astype(bf16)
    on = jnp.concatenate([s.on[f + k] for k in range(per)], 0).astype(bf16)
    s.grads[OUT1 : OUT1 + D, :] += mm(da, on)
    do = mm_nt(eye(local * per), mm(s.w[:, OUT1 : OUT1 + D], da).astype(bf16))
    for k in range(per):
        at = slice(local * k, local * (k + 1))
        s.n1[f + k] = dr[:, at]
        s.nat[f + k, :, 0:D] = do[at]


def group_main(s, low, high, total):
    ident = eye(D)

    def start(i, base):
        don = jnp.concatenate([group_cells(s.nat, 2 * i), group_cells(s.nat, 2 * i + 1)], 0)
        do = mm_nt(ident, don[:, 0:D])
        for k in range(2):
            g = 2 * i + k
            for h in range(HEADS):
                hs = slice(HD * h, HD * (h + 1))
                hl = slice(CELLS * h, CELLS * (h + 1))
                scaled = (do[hs, CELLS * k : CELLS * (k + 1)] * s.inv[g, :, hl]).astype(bf16)
                s.dbd[base + k, hs, hl] = scaled
                part = scaled.astype(f32) * s.og1[g, hs, :].astype(f32)
                s.delta[base + k, :, hl] = jnp.sum(part, 0, keepdims=True)

    def rest(i, k, base):
        g = 2 * i + k
        t = mm(s.vn[g], s.dbd[base + k]) - s.delta[base + k]
        exb = s.expo[g]
        ds = (exb.astype(f32) * t).astype(bf16)
        at = slice(CELLS * k, CELLS * (k + 1))
        for h in range(HEADS):
            hs = slice(HD * h, HD * (h + 1))
            ks = slice(D + HD * h, D + HD * (h + 1))
            vs = slice(2 * D + HD * h, 2 * D + HD * (h + 1))
            hl = slice(CELLS * h, CELLS * (h + 1))
            dq = mm(s.qkv[i, ks, at], ds[:, hl]) * SCALE
            dk = mm_nt(s.qkv[i, hs, at], ds[:, hl]) * SCALE
            dv = mm_nt(s.dbd[base + k, hs, hl], exb[:, hl])
            s.qkv[i, hs, at] = dq.astype(bf16)
            s.qkv[i, ks, at] = dk.astype(bf16)
            s.qkv[i, vs, at] = dv.astype(bf16)

    def both(i, base):
        for k in range(2):
            rest(i, k, base)

    def body(j, _):
        i = low + 2 * j
        start(i + 1, 2)
        both(i, 0)
        start(jnp.minimum(i + 2, total - 1), 0)
        both(i + 1, 2)
        return 0

    if low == 0:
        start(0, 0)
    lax.fori_loop(0, (high - low) // 2, body, 0)


def group_grad(s):
    res = 0.0
    for i in range(s.qkv.shape[0]):
        res = res + mm(s.qkv[i], s.eg[2 * CELLS * i : 2 * CELLS * (i + 1), :])
    s.grads[QKV1 : QKV1 + 3 * D, :] = res[:, 0:D]
    gone = res[:, D:EAUG]
    high = gone.astype(bf16)
    low = (gone - high.astype(f32)).astype(bf16)
    w = s.w[:, QKV1 : QKV1 + 3 * D]
    s.vacc[0, :, 0:16] += mm(w, high) + mm(w, low)


def group_close(s, low, high):
    def close(i, _):
        de = mm(s.w[:, QKV1 : QKV1 + 3 * D], s.qkv[i]).T
        for k in range(2):
            rows = pl.ds(pl.multiple_of((2 * i + k) * SUB, SUB), SUB)
            s.on[:, rows, :] = de[CELLS * k : CELLS * (k + 1)].reshape(F, SUB, D)
        return 0

    lax.fori_loop(low, high, close, 0)


def rows_finish(s):
    def one(f, _):
        absent = s.missing[pl.ds(f, 1), :] > 0
        de = s.n1[f] + s.on[f].T
        s.et[f] = jnp.where(absent, 0.0, de).astype(bf16)
        return 0

    lax.fori_loop(0, F, one, 0, unroll=2)


def adam(param, grad, first, second, average, rate):
    first_new = B1 * first + (1.0 - B1) * grad
    second_new = B2 * second + (1.0 - B2) * grad * grad
    first_hat = first_new * (1.0 / (1.0 - B1**STEP))
    second_hat = second_new * (1.0 / (1.0 - B2**STEP))
    param_new = param - rate * (first_hat / (jnp.sqrt(second_hat) + ADAM_EPS) + DECAY * param)
    average_new = EMA * average + (1.0 - EMA) * param_new
    return param_new, first_new, second_new, average_new


def local_scratch(nr):
    local = ROWS // nr
    fc = F // nr
    groups = local // SUB
    return dict(
        wt=((COLS, D), bf16),
        w=((D, COLS), bf16),
        vect=((D, 16), f32),
        et=((F, D, local), bf16),
        nat=((F, local, EAUG), f32),
        on=((F, local, D), f32),
        eg=((groups * CELLS, EAUG), bf16),
        qkv=((groups // 2, 3 * D, 2 * CELLS), bf16),
        vn=((groups, CELLS, D), bf16),
        expo=((groups, CELLS, WIDE), bf16),
        inv=((groups, 1, WIDE), f32),
        og1=((groups, D, CELLS), bf16),
        n1=((F, D, local), f32),
        rstd1=((F, 1, local), f32),
        qbd=((2, GAUG, WIDE), bf16),
        dbd=((4, D, WIDE), bf16),
        delta=((4, 1, WIDE), f32),
        kaug=((2 * groups, CELLS, 128), bf16),
        pick=((ROWS, KEYS), bf16),
        xt=((D, ROWS), bf16),
        xct=((D, KEYS), bf16),
        kt=((D, KEYS), bf16),
        ka=((HEADS // 2, KEYS, 128), bf16),
        vb=((HEADS // 2, KEYS, 128), bf16),
        sc=((2, KEYS, SPAN), f32),
        top=((2, 8, SPAN), f32),
        va=((HEADS, HD + 16, KEYS), bf16),
        qa=((HEADS, KAUG, ROWS), bf16),
        da=((HEADS, 128, ROWS), bf16),
        ex=((HEADS, KEYS, ROWS), bf16),
        ot=((HEADS, HD + 8, ROWS), f32),
        o2=((D, ROWS), bf16),
        h2b=((D, ROWS), bf16),
        gb=((FFN, ROWS), bf16),
        dub=((FFN, ROWS), bf16),
        dzb=((D, ROWS), bf16),
        da2b=((D, ROWS), bf16),
        dqb=((D, ROWS), bf16),
        dkvb=((2 * D, KEYS), bf16),
        vacc=((10, D, 128), f32),
        grads=((COLS + 32, D), f32),
        hs=((F, D, local), bf16),
        hr=((nr, fc, D, local), bf16),
        gr=((nr, fc, D, local), bf16),
        dr=((F, D, local), bf16),
    )


IN_NAMES = ["cells", "missing", "count", "og", "mat", "vec"]
OUT_NAMES = ["layer", "igrad", "norm", "mgrad", "vgrad"]


def shapes_of(width):
    first = -(-(width + 1) // 16) * 16
    half = -(-(-(-(width + 1) // 2)) // 8) * 8
    return first, half, first + -(-half // 16) * 16


def pack(block, width):
    first, half, total = shapes_of(width)
    rows = block.shape[0]
    low = block[:, 0:128]
    if rows < first:
        low = jnp.concatenate([low, jnp.zeros((first - rows, 128), f32)], 0)
    high = block[:, 128:D]
    high = jnp.concatenate([high, jnp.zeros((2 * half - rows, 64), f32)], 0)
    high = jnp.concatenate([high[0:half], high[half:]], 1)
    if half < total - first:
        high = jnp.concatenate([high, jnp.zeros((total - first - half, 128), f32)], 0)
    return jnp.concatenate([low, high], 0)


def unpack(packed, width, rows):
    first, half, total = shapes_of(width)
    low = packed[0:rows]
    high = packed[first : first + half]
    high = jnp.concatenate([high[:, 0:64], high[0 : rows - half, 64:128]], 0)
    return jnp.concatenate([low, high], 1)


def whole_kernel(nr, n, names, *refs):
    s = Refs(names, refs)
    if not hasattr(s, "kaug"):
        s.kaug = s.sib
    local = ROWS // nr
    fc = F // nr
    width = s.mat.shape[0]
    t = lax.axis_index("table")
    row = lax.axis_index("row")
    me = t * nr + row
    core = lax.rem(t, 2)
    nt = n // nr
    nx, nz = nt // 2, 4
    ny = nr // nz
    x, z, y = t // 2, row // ny, lax.rem(row, ny)
    flat = x * ny + y
    plane = nx * ny
    critical = -(-4 * D // width)
    late = -(-3 * D // width)
    sibling = (t + 1 - 2 * core, row)
    barrier = pltpu.get_barrier_semaphore()

    def place(p):
        return (p // nr, lax.rem(p, nr))

    def core_of(p):
        return lax.rem(p // nr, 2)

    def remote(src, dst, send, recv, device):
        return pltpu.make_async_remote_copy(
            src_ref=src, dst_ref=dst, send_sem=send, recv_sem=recv, device_id=device, device_id_type=MESH
        )

    def others(count, first, body):
        def step(k, _):
            body(lax.rem(first + k, count))
            return 0

        lax.fori_loop(1, count, step, 0)

    def along(j):
        return (t, lax.rem(z + j, nz) * ny + y)

    def across(j):
        q = lax.rem(flat + j, plane)
        return (2 * (q // ny) + core, z * ny + lax.rem(q, ny))

    def on_line(p):
        return ((p // nr) == t) & (lax.rem(p, ny) == y)

    def slots(low, high, want, body):
        def step(p, _):
            @pl.when(want(p))
            def _():
                body(p)

            return 0

        lax.fori_loop(low, high, step, 0)

    def mine(p):
        return core_of(p) == core

    def theirs(p):
        return core_of(p) != core

    def mine_not_me(p):
        return (core_of(p) == core) & (p != me)

    def greet(p):
        q = lax.rem(p, nr)

        @pl.when(((p // nr) == t) | (q == row) | ((core_of(p) == core) & ((q // ny) == z)))
        def _():
            pl.semaphore_signal(barrier, inc=1, device_id=place(p), device_id_type=MESH)

    others(n, me, greet)
    partners = (nr - 1) + (nt - 1) + (nx - 1) * (ny - 1)

    stage = pltpu.make_async_copy(s.cells, s.hs, s.c_sem)
    stage.start()
    s.wr[me] = pack(s.mat[...], width).astype(bf16)
    v = jnp.concatenate([s.vec[...], jnp.zeros((128 - 10, D), f32)], 0)
    v = jnp.concatenate([v, jnp.zeros((128, 256 - D), f32)], 1).T
    s.vect[...] = v[0:D, 0:16]
    pl.semaphore_wait(barrier, partners)

    def weights(slot, send, device):
        return remote(s.wr.at[slot], s.wr.at[slot], send, s.w_recv.at[slot], device)

    def by_line(j):
        return weights(me, s.wz_send.at[j], along(j))

    def by_plane(slot, j):
        return weights(slot, s.wp_send.at[slot, j], across(j))

    def by_core(slot):
        return weights(slot, s.wc_send.at[slot], sibling)

    def arrive(slot):
        weights(slot, s.wc_send.at[slot], sibling).wait_recv()

    def line_slot(j):
        return t * nr + lax.rem(z + j, nz) * ny + y

    def to_all(slot):
        for j in range(1, plane):
            by_plane(slot, j).start()
        by_core(slot).start()

    def line_arrivals(want):
        for j in range(1, nz):
            p = line_slot(j)

            @pl.when(want(p))
            def _(p=p):
                arrive(p)
                to_all(p)

    def plane_arrivals(want):
        def step(i, _):
            q = lax.rem(flat + 1 + i // nz, plane)
            p = (2 * (q // ny) + core) * nr + lax.rem(i, nz) * ny + lax.rem(q, ny)

            @pl.when(want(p))
            def _():
                arrive(p)
                by_core(p).start()

            return 0

        lax.fori_loop(0, (plane - 1) * nz, step, 0)

    def is_critical(p):
        return p < critical

    def is_other(p):
        return p >= critical

    order = [lax.rem(z + 2, nz), 3 - z, z + 1 - 2 * lax.rem(z, 2), z]

    def peers(body):
        for zz in order:
            for yy in range(ny):
                p = zz * ny + yy

                @pl.when(p != row)
                def _(p=p):
                    body(p)

    def unpack_slots(low, high):
        for p in range(low, high):
            s.grads[p * width : (p + 1) * width, :] = unpack(s.wr[p].astype(f32), width, width)

    def spread(low, high):
        for k in range(low // 128, high // 128):
            piece = s.grads[128 * k : 128 * (k + 1), :]
            s.wt[128 * k : 128 * (k + 1), :] = piece.astype(bf16)
            s.w[:, 128 * k : 128 * (k + 1)] = piece.T.astype(bf16)

    def give_grad(p, col):
        return remote(
            s.og.at[col * nr + p], s.gr.at[row, col], s.g_send.at[col, p], s.g_recv.at[col, row], (t, p)
        )

    def got_grad(p, col):
        return remote(
            s.og.at[col * nr + p], s.gr.at[p, col], s.g_send.at[col, p], s.g_recv.at[col, p], (t, p)
        )

    def publish():
        for j in range(1, nz):
            by_line(j).start()
        to_all(me)

    publish()
    stage.wait()
    embed(s, local)
    line_arrivals(is_critical)
    group_setup(s)
    s.vacc[...] = jnp.zeros(s.vacc.shape, f32)
    plane_arrivals(is_critical)

    line_arrivals(is_other)

    peers(lambda p: give_grad(p, 0).start())
    slots(0, critical, theirs, arrive)
    unpack_slots(0, critical)
    spread(0, 4 * D)

    group_forward(s, local)

    def give(p, col):
        return remote(
            s.hs.at[col * nr + p], s.hr.at[row, col], s.h_send.at[col, p], s.h_recv.at[col, row], (t, p)
        )

    def got(p, col):
        return remote(
            s.hs.at[col * nr + p], s.hr.at[p, col], s.h_send.at[col, p], s.h_recv.at[col, p], (t, p)
        )

    for col in range(fc):
        for zz in order:
            rows_norm(s, col * nr + zz * ny, ny)
            for yy in range(ny):
                q = zz * ny + yy

                @pl.when(q != row)
                def _(q=q, col=col):
                    give(q, col).start()

        s.hr[row, col] = s.hs[col * nr + row]
    for col in range(1, fc):
        peers(lambda p, col=col: give_grad(p, col).start())
    own = [pltpu.make_async_copy(s.og.at[col * nr + row], s.gr.at[row, col], s.o_sem.at[col]) for col in range(fc)]
    for c in own:
        c.start()
    for c in own:
        c.wait()
    plane_arrivals(is_other)
    make_pick(s)
    s.da[...] = jnp.zeros(s.da.shape, bf16)
    slots(critical, n, theirs, arrive)
    unpack_slots(critical, n)
    spread(4 * D, COLS)
    s.grads[...] = jnp.zeros(s.grads.shape, f32)

    def back_layer(p, col):
        return remote(
            s.et.at[col * nr + p], s.layer.at[col * nr + row], s.l_send.at[col, p], s.l_recv.at[col * nr + row], (t, p)
        )

    def back_grad(p, col):
        return remote(
            s.hs.at[col * nr + p], s.dr.at[col * nr + row], s.d_send.at[col, p], s.d_recv.at[col * nr + row], (t, p)
        )

    def sent_rows(p):
        for c in range(fc):
            give(p, c).wait_send()

    def keep(col):
        return pltpu.make_async_copy(s.et.at[col * nr + row], s.layer.at[col * nr + row], s.k_sem.at[col])

    for col in range(fc):
        others(nr, row, lambda p: got(p, col).wait_recv())
        column_project(s, col, nr)
        column_forward(s)
        others(nr, row, lambda p: got_grad(p, col).wait_recv())
        column_cells(s, col, nr)
        peers(lambda p, col=col: back_layer(p, col).start())
        keep(col).start()
        column_backward(s)
        if col == 0:
            peers(sent_rows)

        def finished(p, col=col):
            @pl.when(p != row)
            def _():
                back_grad(p, col).start()

        column_finish(s, col, nr, order, finished)
        column_grads(s)
        s.dr[col * nr + row] = s.hs[col * nr + row]

    def totals(v):
        if v >= 10:
            return None
        acc = s.vacc[v]
        high = acc.astype(bf16)
        low = (acc - high.astype(f32)).astype(bf16)
        ones = jnp.ones((16, 128), bf16)
        return (mm_nt(ones, high) + mm_nt(ones, low))[0:1]

    def piece(p, extra=None):
        block = s.grads[p * width : (p + 1) * width, :]
        last = jnp.zeros((8, D), f32) if extra is None else jnp.broadcast_to(extra, (8, D))
        last = jnp.where(iota((8, D), 0) == 0, last, 0.0)
        s.wr[p] = pack(jnp.concatenate([block, last], 0)[0 : width + 1], width).astype(bf16)

    def exchange(p):
        return remote(s.wr.at[p], s.sib.at[p], s.x_send.at[p], s.x_recv.at[p], sibling)

    def inward(p, j, k):
        return remote(s.sib.at[p], s.pin.at[j, k], s.p_send.at[p], s.p_recv.at[j, k], across(j))

    def outward(j):
        k = lax.rem(z + j, nz)
        return remote(s.two.at[k], s.zin.at[j], s.z_send.at[j], s.z_recv.at[j], along(j))

    def steps_to(p):
        q = (p // nr // 2) * ny + lax.rem(p, ny)
        return lax.rem(q - flat + plane, plane)

    def z_of(p):
        return lax.rem(p, nr) // ny

    def to_sibling(low, high):
        slots(low, high, theirs, lambda p: exchange(p).start())

    def to_plane(low, high):
        def send(p):
            exchange(p).wait_recv()
            s.sib[p] = (s.wr[p].astype(f32) + s.sib[p].astype(f32)).astype(bf16)

            @pl.when(jnp.logical_not(on_line(p)))
            def _():
                inward(p, steps_to(p), z_of(p)).start()

        slots(low, high, mine, send)

    def to_line(low, high):
        def send(p):
            k = z_of(p)
            total = s.sib[p].astype(f32)
            for j in range(1, plane):
                inward(p, j, k).wait_recv()
                total = total + s.pin[j, k].astype(f32)
            s.two[k] = total.astype(bf16)

            @pl.when(p != me)
            def _():
                outward(lax.rem(k - z + nz, nz)).start()

        slots(low, high, on_line, send)

    def tell(src, p):
        return remote(s.note, s.notes.at[src], s.n_send.at[p], s.n_recv.at[src], (t, p))

    def share(j):
        tt = lax.rem(t + j, nt)
        own = s.notes.at[pl.ds(t * nr, nr)]
        return remote(own, own, s.s_send.at[j], s.s_recv.at[t], (tt, row))

    def shared(j):
        tt = lax.rem(t + j, nt)
        other = s.notes.at[pl.ds(tt * nr, nr)]
        return remote(other, other, s.s_send.at[j], s.s_recv.at[tt], (tt, row))

    def spread_notes():
        others(nr, row, lambda p: tell(t * nr + p, p).wait_recv())
        for j in range(1, nt):
            share(j).start()

    def settle():
        total = s.two[z].astype(f32)
        for j in range(1, nz):
            outward(j).wait_recv()
            total = total + s.zin[j].astype(f32)
        total = unpack(total, width, width + 1)
        vec_row = total[width : width + 1, :]
        grad = total[0:width]
        s.mgrad[...] = grad
        squares = jnp.sum(jnp.sum(grad * grad, 0, keepdims=True), 1, keepdims=True)
        tail = jnp.concatenate([vec_row[:, 128:D], jnp.broadcast_to(squares, (1, 64))], 1)
        s.note[...] = jnp.concatenate([vec_row[:, 0:128], tail], 0)
        s.notes[me] = s.note[...]
        peers(lambda p: tell(me, p).start())

    for j in range(1, nz):
        by_line(j).wait_send()

    def left(p):
        by_core(p).wait_send()

        @pl.when(on_line(p))
        def _():
            for j in range(1, plane):
                by_plane(p, j).wait_send()

    slots(0, n, mine, left)
    for p in range(critical, n):
        piece(p, totals(p))
    to_sibling(critical, n)

    for col in range(fc):
        if col == fc - 1:
            to_plane(critical, n)
        for zz in order[::-1]:
            for yy in range(ny):
                q = zz * ny + yy

                @pl.when(q != row)
                def _(q=q, col=col):
                    f = col * nr + q
                    remote(s.hs.at[f], s.dr.at[f], s.d_send.at[col, q], s.d_recv.at[f], (t, q)).wait_recv()

            rows_norm_back(s, col * nr + zz * ny, ny)
    for p in range(late, critical):
        piece(p, totals(p))
    to_sibling(late, critical)
    pairs = local // SUB // 2
    group_main(s, 0, pairs // 2, pairs)
    to_line(critical, n)
    to_plane(late, critical)
    group_main(s, pairs // 2, pairs, pairs)
    to_line(late, critical)
    group_grad(s)
    for p in range(late):
        piece(p, totals(p))
    to_sibling(0, late)

    first_early = -(-late // nr)

    @pl.when(t >= first_early)
    def _():
        settle()

    most = pairs * 5 // 8
    group_close(s, 0, most)
    to_plane(0, late)
    group_close(s, most, pairs)

    @pl.when(t >= first_early)
    def _():
        spread_notes()

    for col in range(fc):
        peers(lambda p, col=col: back_layer(p, col).wait_send())
        keep(col).wait()
    rows_finish(s)
    result = pltpu.make_async_copy(s.et, s.igrad, s.c_sem)
    result.start()
    to_line(0, late)

    @pl.when(t < first_early)
    def _():
        settle()
        spread_notes()

    for j in range(1, nt):
        shared(j).wait_recv()
    squares = lax.fori_loop(0, n, lambda k, x: x + s.notes[k, 1:2, 64:65], jnp.zeros((1, 1), f32))
    vec_total = jnp.concatenate(
        [jnp.concatenate([s.notes[p, 0:1, :], s.notes[p, 1:2, 0:64]], 1) for p in range(10)], 0
    )
    squares = squares + jnp.sum(jnp.sum(vec_total * vec_total, 0, keepdims=True), 1, keepdims=True)
    norm = jnp.sqrt(squares)
    s.norm[...] = norm
    factor = CLIP / jnp.maximum(norm, CLIP)
    s.mgrad[...] = s.mgrad[...] * factor
    s.vgrad[...] = vec_total * factor

    result.wait()
    for j in range(1, nz):
        outward(j).wait_send()

    def departed(p):
        @pl.when(jnp.logical_not(on_line(p)))
        def _():
            inward(p, steps_to(p), z_of(p)).wait_send()

    slots(0, n, mine, departed)
    slots(0, n, theirs, lambda p: exchange(p).wait_send())
    peers(lambda p: tell(me, p).wait_send())
    for j in range(1, nt):
        share(j).wait_send()

    def sent_row(p):
        for col in range(fc):
            give_grad(p, col).wait_send()
            back_grad(p, col).wait_send()
            f = col * nr + p
            remote(s.et.at[col * nr + p], s.layer.at[f], s.l_send.at[col, p], s.l_recv.at[f], (t, p)).wait_recv()

    others(nr, row, sent_row)


def update_kernel(*refs):
    ins, outs = refs[0:12], refs[13:23]
    refs[23][...] = refs[12][...]
    held, made = refs[24:36], refs[36:44]
    in_sem, out_sem = refs[44:46]
    loads = [pltpu.make_async_copy(a, b, in_sem.at[k]) for k, (a, b) in enumerate(zip(ins, held))]
    sources = held[0:2] + made
    stores = [pltpu.make_async_copy(a, b, out_sem.at[k]) for k, (a, b) in enumerate(zip(sources, outs))]
    for load in loads[2:] + loads[:2]:
        load.start()
    for load in loads[2:]:
        load.wait()
    w, grad, m1, m2, m3, v, vgrad, v1, v2, v3 = (ref[...] for ref in held[2:12])
    for k, value in enumerate(adam(w, grad, m1, m2, m3, RATE) + adam(v, vgrad, v1, v2, v3, VEC_RATE)):
        made[k][...] = value
        stores[k + 2].start()
    for load, store in zip(loads[:2], stores[:2]):
        load.wait()
        store.start()
    for store in stores:
        store.wait()


def on_device(nr, n, cells, missing, train_counts, out_grad, matrices, vectors, m1, m2, m3, v1, v2, v3):
    local = ROWS // nr
    fc = F // nr
    width = matrices.shape[1]
    packed = (shapes_of(width)[2], 128)
    plane = n // 2 // 4
    sds = jax.ShapeDtypeStruct
    big = sds((F, D, local), bf16)
    dma = pltpu.SemaphoreType.DMA
    scratch = {k: pltpu.VMEM(shape, dtype) for k, (shape, dtype) in local_scratch(nr).items()}
    scratch.update(
        wr=pltpu.VMEM((n,) + packed, bf16),
        sib=pltpu.VMEM((n,) + packed, bf16),
        pin=pltpu.VMEM((plane, 4) + packed, bf16),
        two=pltpu.VMEM((4,) + packed, bf16),
        zin=pltpu.VMEM((4,) + packed, bf16),
        note=pltpu.VMEM((2, 128), f32),
        notes=pltpu.VMEM((n, 2, 128), f32),
        w_recv=dma((n,)),
        c_sem=dma(()),
        o_sem=dma((fc,)),
        k_sem=dma((fc,)),
        wz_send=dma((4,)),
        wp_send=dma((n, plane)),
        wc_send=dma((n,)),
        h_send=dma((fc, nr)),
        h_recv=dma((fc, nr)),
        g_send=dma((fc, nr)),
        g_recv=dma((fc, nr)),
        l_send=dma((fc, nr)),
        l_recv=dma((F,)),
        d_send=dma((fc, nr)),
        d_recv=dma((F,)),
        x_send=dma((n,)),
        x_recv=dma((n,)),
        p_send=dma((n,)),
        p_recv=dma((plane, 4)),
        z_send=dma((4,)),
        z_recv=dma((4,)),
        n_send=dma((nr,)),
        n_recv=dma((n,)),
        s_send=dma((n // nr,)),
        s_recv=dma((n // nr,)),
    )
    shared = scratch["sib"].shape == scratch["kaug"].shape
    if shared:
        del scratch["kaug"]
    names = IN_NAMES + OUT_NAMES + list(scratch)
    in_specs = [VMEM] * 6
    in_specs[0] = in_specs[3] = pl.BlockSpec(memory_space=pl.ANY)
    in_specs[2] = pl.BlockSpec(memory_space=pltpu.SMEM)
    layer, igrad, norm, mgrad, vgrad = pl.pallas_call(
        functools.partial(whole_kernel, nr, n, names),
        out_shape=[big, big, sds((1, 1), f32), sds((width, D), f32), sds((10, D), f32)],
        in_specs=in_specs,
        out_specs=[pl.BlockSpec(memory_space=pl.ANY)] * 2 + [VMEM] * 3,
        scratch_shapes=list(scratch.values()),
        name="whole",
        compiler_params=pltpu.CompilerParams(
            collective_id=0, has_side_effects=True, vmem_limit_bytes=63 * 2**20
        ),
    )(
        cells[0].transpose(1, 2, 0),
        missing[0].T,
        train_counts,
        out_grad[0].transpose(1, 2, 0),
        matrices.T,
        vectors,
    )
    mat = sds((width, D), f32)
    vec = sds((10, D), f32)
    anywhere = pl.BlockSpec(memory_space=pl.ANY)
    held = [big] * 2 + [mat] * 5 + [vec] * 5
    made = [mat] * 4 + [vec] * 4
    layer, igrad, *rest, norm = pl.pallas_call(
        update_kernel,
        out_shape=[big, big] + made + [sds((1, 1), f32)],
        in_specs=[anywhere] * 12 + [VMEM],
        out_specs=[anywhere] * 10 + [VMEM],
        scratch_shapes=[pltpu.VMEM(x.shape, x.dtype) for x in held + made] + [dma((12,)), dma((10,))],
        name="update",
    )(layer, igrad, matrices.T, mgrad, m1.T, m2.T, m3.T, vectors, vgrad, v1, v2, v3, norm)
    back = (2, 0, 1)
    return (
        layer.transpose(back)[None],
        igrad.transpose(back)[None],
        norm[0, 0],
        *[m.T for m in rest[:4]],
        *rest[4:],
    )


def solution(mesh):
    rows = P("table", "row", None, None)
    shard = P(None, ("table", "row"))
    nr = mesh.shape["row"]
    return jax.shard_map(
        functools.partial(on_device, nr, nr * mesh.shape["table"]),
        mesh=mesh,
        in_specs=(rows, P("table", "row", None), P("table"), rows, shard, P(), shard, shard, shard, P(), P(), P()),
        out_specs=(rows, rows, P(), shard, shard, shard, shard, P(), P(), P(), P()),
        check_vma=False,
    )
```
